32 devices in a mesh: row: 8 (over z, x), col: 4 (over y, core).
Axes of the slice: x: 2, y: 2, z: 4, core: 2. Of those that a mesh axis runs over, the one named last changes fastest.
Arguments:
- residual: bfloat16 [1024, 7168], P('col', 'row'), may hold values from -30 to 30
- attn_gain: float32 [7168], P('row'), may hold values from 0.25 to 1.75
- w_query: bfloat16 [7168, 7168], P('row', 'col'), may hold values from -1 to 1
- w_key: bfloat16 [7168, 1024], P('row', 'col'), may hold values from -11 to 11
- value_weight: bfloat16 [7168, 1024], P('row', 'col'), may hold values from -0.0625 to 0.0625
- w_out: bfloat16 [7168, 7168], P('col', 'row'), may hold values from -0.0625 to 0.0625
- mlp_gain: float32 [7168], P('col'), may hold values from 0.25 to 1.75
- w_gate: bfloat16 [7168, 20480], P('col', 'row'), may hold values from -0.0625 to 0.0625
- w_up: bfloat16 [7168, 20480], P('col', 'row'), may hold values from -0.0625 to 0.0625
- w_down: bfloat16 [20480, 7168], P('row', 'col'), may hold values from -0.0390625 to 0.0390625
- segment_ids: int32 [1024], replicated, may hold values from 0 to 7, never falling along the last dimension, each value on 1 to 512 neighbouring positions
- page_table: int32 [64], replicated, may hold values from 0 to 63, each once
Outputs:
- output: bfloat16 [1024, 7168], P('row', 'col')
- key_cache_pages: bfloat16 [64, 16, 1024], P('row', None, 'col')
- value_cache_pages: bfloat16 [64, 16, 1024], P('row', None, 'col')
The draws below stay inside these ranges and needn't reach their ends.
Inputs may be any that keep to these rules, and one draw needn't show every extreme that they name: `segment_ids`: document numbers never fall along the stream; each of the 8 documents holds 1 to 512 tokens and one holds exactly 512. A permutation: the tokens b * 16 to b * 16 + 15 go to cache slot page_table[b].
All inputs are finite; a program needn't handle non-finite values.
Results may differ from the reference program's by a relative error of at most 0.035.
Values may be sent and summed in bfloat16 or wider, within the bound.
No kernel may reach another device: no remote copies, remote signals or barrier semaphores. Data moves between devices by JAX's collectives and lax.ppermute only.
A program may use at most 128 MiB of HBM per device.

```python
import math
import jax
import jax.numpy as jnp
import numpy as np
from jax import lax

MODEL_DIM = 7168
QUERY_HEADS = 56
KEY_VALUE_HEADS = 8
HEAD_SIZE = 128
FF = 20480
PAGE_TOKENS = 16
NSEG = 8
TOKEN_COUNT = 1024
DOC_MOST = 512
PAGE_COUNT = 64
N_ROW = 8
N_COL = 4


def draw_residual(key, part):
    subkeys = jax.random.split(jax.random.fold_in(key, 101), 4)
    columns = jnp.arange(MODEL_DIM, dtype=jnp.float32) / MODEL_DIM
    base_draw = jnp.clip(jax.random.normal(subkeys[0], (TOKEN_COUNT, MODEL_DIM), jnp.float32), -2.5, 2.5)
    column_ramp = jnp.sqrt((0.5 + columns) / 1.5)
    row_scale = jnp.exp(jax.random.uniform(subkeys[2], (TOKEN_COUNT, 1), jnp.float32, -1.15, 1.15))
    column_scale = jnp.exp(jax.random.uniform(subkeys[3], (1, MODEL_DIM), jnp.float32, -1.15, 1.15)) * column_ramp[None, :]
    return (base_draw * row_scale * column_scale).astype(jnp.bfloat16)


def query_projected(key):
    gaussian_sample = jax.random.normal(jax.random.fold_in(key, 202), (MODEL_DIM, QUERY_HEADS * HEAD_SIZE), jnp.float32)
    return jnp.clip(gaussian_sample, -5.0, 5.0) * MODEL_DIM ** (-0.5)


def draw_w_query(key, part):
    return query_projected(key).astype(jnp.bfloat16)


def draw_w_key(key, part):
    gaussian_sample = jax.random.normal(jax.random.fold_in(key, 303), (MODEL_DIM, KEY_VALUE_HEADS, HEAD_SIZE), jnp.float32)
    current_page = jnp.clip(gaussian_sample, -5.0, 5.0) * MODEL_DIM ** (-0.5)
    return current_page.reshape(MODEL_DIM, KEY_VALUE_HEADS * HEAD_SIZE).astype(jnp.bfloat16)


def block_levels(own_key, dims, cuts, smallest, largest):
    def one(axis_at, blocks):
        steps = jax.random.uniform(jax.random.fold_in(jax.random.fold_in(own_key, 6), axis_at), (blocks,), jnp.float32, smallest / len(cuts), largest / len(cuts))
        return jnp.repeat(jnp.exp(steps), dims[axis_at] // blocks).reshape((-1,) + (1,) * (len(dims) - axis_at - 1))

    factor_of = one(*cuts[0])
    for cut in cuts[1:]:
        factor_of = factor_of * one(*cut)
    return factor_of


def length_profile(amount, total, reach, slope):
    loads = [(1 << 20) // math.isqrt(rank ** slope) + 1 for rank in range(2, amount + 1)]
    rest, given = total - reach - (amount - 1), [1] * (amount - 1)
    while rest > 0:
        movable = [i for i in range(amount - 1) if given[i] < reach]
        pool, budget = sum([loads[i] for i in movable]), rest
        for i in movable:
            addition = min(reach - given[i], max(1, budget * loads[i] // pool), rest)
            given[i] = given[i] + addition
            rest = rest - addition
    return np.array([reach] + given)


def uneven_parts(stream_key, amount, total, limit, slope):
    if amount == 2:
        one = jax.random.randint(stream_key, (), max(1, total - limit), min(limit, total - 1) + 1)
        return jnp.stack([one, total - one])
    tallies = jnp.asarray(length_profile(amount, total, limit, slope), jnp.int32)
    couples = (amount - 1) // 2
    donor, receiver = tallies[1:1 + 2 * couples:2], tallies[2:2 + 2 * couples:2]
    room = jnp.minimum(donor - 1, limit - receiver)
    shifted = jax.random.randint(jax.random.fold_in(stream_key, 1), (couples,), 0, 1 << 20) % (room + 1)
    tallies = tallies.at[1:1 + 2 * couples:2].set(donor - shifted).at[2:2 + 2 * couples:2].set(receiver + shifted)
    return tallies[jax.random.permutation(jax.random.fold_in(stream_key, 2), amount)]


def noise(stream_key, dims, deviation, limit, cuts=(), kind=jnp.bfloat16):
    array = jax.random.normal(stream_key, dims, jnp.float32) * deviation
    if len(cuts) > 0:
        array = block_levels(stream_key, dims, cuts, -0.22, 0.18) * array
    return jnp.clip(array, min=-limit, max=limit).astype(kind)


def setup_inputs(seed: int = 0) -> dict:
    key_list = jax.random.split(jax.random.key(seed), 13)
    return {
        "residual": draw_residual(jax.random.fold_in(key_list[12], 71), 0),
        "attn_gain": jnp.clip(1.0 + 0.15 * jax.random.normal(key_list[1], (MODEL_DIM,), jnp.float32), 0.25, 1.75),
        "w_query": draw_w_query(jax.random.fold_in(key_list[12], 71), 0),
        "w_key": draw_w_key(jax.random.fold_in(key_list[12], 71), 0),
        "value_weight": noise(key_list[4], (MODEL_DIM, KEY_VALUE_HEADS * HEAD_SIZE), MODEL_DIM ** -0.5, 0.0625, ((0, 8), (1, 4))),
        "w_out": noise(key_list[5], (QUERY_HEADS * HEAD_SIZE, MODEL_DIM), (QUERY_HEADS * HEAD_SIZE) ** -0.5, 0.0625, ((0, 4), (1, 8))),
        "mlp_gain": jnp.clip(1.0 + 0.15 * jax.random.normal(key_list[6], (MODEL_DIM,), jnp.float32), 0.25, 1.75),
        "w_gate": noise(key_list[7], (MODEL_DIM, FF), MODEL_DIM ** -0.5, 0.0625, ((0, 4), (1, 8))),
        "w_up": noise(key_list[8], (MODEL_DIM, FF), MODEL_DIM ** -0.5, 0.0625, ((0, 4), (1, 8))),
        "w_down": noise(key_list[9], (FF, MODEL_DIM), FF ** -0.5, 0.0390625, ((0, 8), (1, 4))),
        "segment_ids": jnp.searchsorted(jnp.cumsum(uneven_parts(key_list[10], NSEG, TOKEN_COUNT, DOC_MOST, 2)), jnp.arange(TOKEN_COUNT), side="right").astype(jnp.int32),
        "page_table": jax.random.permutation(key_list[11], PAGE_COUNT).astype(jnp.int32),
    }


ROPE_BASE = 5000000.0
EPSILON = 1e-05
NEGATIVE = -1e+30

def rotary_apply(block, token_positions):
    half_width = block.shape[-1] // 2
    frequency = ROPE_BASE ** (-2.0 * jnp.arange(half_width, dtype=jnp.float32) / block.shape[-1])
    angles = token_positions.astype(jnp.float32)[:, None] * frequency[None, :]
    cosine = jnp.cos(angles)[:, None, :]
    sine_part = jnp.sin(angles)[:, None, :]
    first_half = block[..., :half_width]
    second = block[..., half_width:]
    return jnp.concatenate([first_half * cosine - second * sine_part, second * cosine + first_half * sine_part], axis=-1)

def blocked_product(left, weight, parts):
    part_width = left.shape[1] // parts

    def add_part(step_index, running):
        begin_at = (step_index * part_width).astype(jnp.int32)
        piece_block = lax.dynamic_slice_in_dim(left, begin_at, part_width, 1)
        row_block = lax.dynamic_slice_in_dim(weight, begin_at, part_width, 0)
        part_term = jnp.dot(piece_block, row_block, preferred_element_type=jnp.float32).astype(jnp.bfloat16)
        part_term = lax.optimization_barrier(part_term)
        return running + part_term.astype(jnp.float32)
    initial = jnp.zeros((left.shape[0], weight.shape[1]), jnp.float32)
    return lax.fori_loop(0, parts, add_part, initial)

def norm_scale(stream):
    widened = stream.astype(jnp.float32)
    return lax.rsqrt(lax.optimization_barrier(jnp.sum(widened * widened, axis=1)) / MODEL_DIM + EPSILON)

def reference(residual, attn_gain, w_query, w_key, value_weight, w_out, mlp_gain, w_gate, w_up, w_down, segment_ids, page_table):
    query_group_width = QUERY_HEADS // KEY_VALUE_HEADS
    attn_scale = norm_scale(residual)[:, None]
    scaled = (residual.astype(jnp.float32) * attn_gain[None, :]).astype(jnp.bfloat16)
    query_heads_rows = blocked_product(scaled, w_query, N_ROW) * attn_scale
    projected_key_rows = blocked_product(scaled, w_key, N_ROW) * attn_scale
    projected_value_rows = (blocked_product(scaled, value_weight, N_ROW) * attn_scale).astype(jnp.bfloat16)
    token_index = jnp.arange(TOKEN_COUNT, dtype=jnp.int32)
    starts = lax.optimization_barrier(jnp.sum((segment_ids[None, :] < segment_ids[:, None]).astype(jnp.int32), axis=1))
    token_positions = token_index - starts
    query_heads_rows = rotary_apply(query_heads_rows.reshape(TOKEN_COUNT, QUERY_HEADS, HEAD_SIZE), token_positions).astype(jnp.bfloat16)
    projected_key_rows = rotary_apply(projected_key_rows.reshape(TOKEN_COUNT, KEY_VALUE_HEADS, HEAD_SIZE), token_positions).astype(jnp.bfloat16)
    key_mask = (segment_ids[None, :] == segment_ids[:, None]) & (token_index[None, :] <= token_index[:, None])
    grouped_queries = jnp.transpose(query_heads_rows.reshape(TOKEN_COUNT, KEY_VALUE_HEADS, query_group_width, HEAD_SIZE), (1, 0, 2, 3))
    per_key = jnp.transpose(projected_key_rows, (1, 0, 2))
    value_per_head = jnp.transpose(projected_value_rows.reshape(TOKEN_COUNT, KEY_VALUE_HEADS, HEAD_SIZE), (1, 0, 2))

    def one_head(head_items):
        query_block, key_block, value_block = head_items
        scores = jnp.einsum('tgd,sd->gts', query_block.astype(jnp.float32), key_block.astype(jnp.float32)) * HEAD_SIZE ** (-0.5)
        scores = jnp.where(key_mask[None], scores, NEGATIVE)
        peak_score = lax.optimization_barrier(jnp.max(scores, axis=2, keepdims=True))
        weights = jnp.where(key_mask[None], jnp.exp(scores - peak_score), 0.0).astype(jnp.bfloat16)
        weight_sum = lax.optimization_barrier(jnp.sum(weights.astype(jnp.float32), axis=2))
        mixture = jnp.einsum('gts,sd->tgd', weights.astype(jnp.float32), value_block.astype(jnp.float32))
        return (mixture / jnp.transpose(weight_sum)[:, :, None]).astype(jnp.bfloat16)
    attended = lax.map(one_head, (grouped_queries, per_key, value_per_head))
    attended = jnp.transpose(attended, (1, 0, 2, 3)).reshape(TOKEN_COUNT, QUERY_HEADS * HEAD_SIZE)
    hidden_stream = (residual.astype(jnp.float32) + blocked_product(attended, w_out, N_COL)).astype(jnp.bfloat16)
    mlp_scale = norm_scale(hidden_stream)[:, None]
    scaled_mid = (hidden_stream.astype(jnp.float32) * mlp_gain[None, :]).astype(jnp.bfloat16)
    gate = blocked_product(scaled_mid, w_gate, N_COL) * mlp_scale
    upward = blocked_product(scaled_mid, w_up, N_COL) * mlp_scale
    hidden = (jax.nn.silu(gate) * upward).astype(jnp.bfloat16)
    output = (hidden_stream.astype(jnp.float32) + blocked_product(hidden, w_down, N_ROW)).astype(jnp.bfloat16)
    slot_page_index = jnp.zeros((PAGE_COUNT,), jnp.int32).at[page_table].set(jnp.arange(PAGE_COUNT, dtype=jnp.int32))
    key_cache_pages = projected_key_rows.reshape(PAGE_COUNT, PAGE_TOKENS, KEY_VALUE_HEADS * HEAD_SIZE)[slot_page_index]
    value_cache_pages = projected_value_rows.reshape(PAGE_COUNT, PAGE_TOKENS, KEY_VALUE_HEADS * HEAD_SIZE)[slot_page_index]
    return (output, key_cache_pages, value_cache_pages)
```

```python
import jax
import jax.numpy as jnp
from jax import lax
from jax.sharding import PartitionSpec as P

HEAD_SIZE = 128
ROPE_BASE = 5000000.0
EPSILON = 1e-05
NEGATIVE = -1e30
PARTS = 2


def ring_of_rows(rows):
    depth = 4 if rows % 4 == 0 else 1
    width = rows // depth
    walk = []
    for x in range(width):
        zs = range(depth) if x % 2 == 0 else reversed(range(depth))
        walk += [z * width + x for z in zs]
    return walk


class Ring:
    def __init__(self, axis, walks, place):
        self.axis = axis
        self.size = len(walks[0])
        total = sum(len(walk) for walk in walks)
        members = [None] * total
        for walk in walks:
            for i, who in enumerate(walk):
                members[who] = [j for j in range(self.size)], i
        n = self.size
        self.right = [(w[i], w[(i + 1) % n]) for w in walks for i in range(n)]
        self.left = [(w[(i + 1) % n], w[i]) for w in walks for i in range(n)]
        self.spot = jnp.array([members[who][1] for who in range(total)], jnp.int32)[place]

    def send(self, block, pairs):
        return lax.ppermute(block, self.axis, pairs)

    def at(self, offset):
        return lax.rem(self.spot + (offset % self.size), self.size)

    def reduce_scatter(self, take):
        n, half = self.size, self.size // 2
        if n == 1:
            return take(0).astype(jnp.float32)
        if n == 2:
            got = self.send(take(1).astype(jnp.bfloat16), self.right)
            return take(0).astype(jnp.float32) + got.astype(jnp.float32)
        far = take(half).astype(jnp.bfloat16)
        cut = far.shape[0] // 2
        going_right = self.send(far[:cut], self.right).astype(jnp.float32)
        going_left = self.send(far[cut:], self.left).astype(jnp.float32)
        for step in range(half - 1, 0, -1):
            one = take(step).astype(jnp.float32)
            two = take(-step).astype(jnp.float32)
            if step == half - 1:
                one = jnp.concatenate([one[:cut] + going_right, one[cut:]], axis=0)
                two = jnp.concatenate([two[:cut], two[cut:] + going_left], axis=0)
            else:
                one = one + going_right
                two = two + going_left
            going_right = self.send(one.astype(jnp.bfloat16), self.right).astype(jnp.float32)
            going_left = self.send(two.astype(jnp.bfloat16), self.left).astype(jnp.float32)
        return take(0).astype(jnp.float32) + going_right + going_left

    def all_gather(self, block):
        n, half = self.size, self.size // 2
        if n == 1:
            return [(0, block)]
        if n == 2:
            return [(0, block), (1, self.send(block, self.right))]
        found = [(0, block)]
        from_left = from_right = block
        for step in range(1, half):
            from_left = self.send(from_left, self.right)
            from_right = self.send(from_right, self.left)
            found += [(-step, from_left), (step, from_right)]
        cut = block.shape[0] // 2
        far = jnp.concatenate(
            [self.send(from_left[:cut], self.right), self.send(from_right[cut:], self.left)], axis=0
        )
        return found + [(half, far)]


def place_blocks(shape, dtype, placed):
    buffer = jnp.zeros(shape, dtype)
    for start, block in placed:
        buffer = lax.dynamic_update_slice(buffer, block, start)
    return buffer


def rotary_tables(token_positions):
    half_width = HEAD_SIZE // 2
    frequency = ROPE_BASE ** (-2.0 * jnp.arange(half_width, dtype=jnp.float32) / HEAD_SIZE)
    angles = token_positions.astype(jnp.float32)[:, None] * frequency[None, :]
    return jnp.cos(angles)[:, None, :], jnp.sin(angles)[:, None, :]


def rotary_apply(block, tables):
    cosine, sine_part = tables
    half_width = block.shape[-1] // 2
    first_half = block[..., :half_width]
    second = block[..., half_width:]
    return jnp.concatenate(
        [first_half * cosine - second * sine_part, second * cosine + first_half * sine_part],
        axis=-1,
    )


def dot32(a, b):
    return jnp.dot(a, b, preferred_element_type=jnp.float32)


def per_device(
    residual,
    attn_gain,
    w_query,
    w_key,
    value_weight,
    w_out,
    mlp_gain,
    w_gate,
    w_up,
    w_down,
    segment_ids,
    page_table,
):
    rows, cols = lax.axis_size("row"), lax.axis_size("col")
    row_place, col_place = lax.axis_index("row"), lax.axis_index("col")
    lanes = cols // 2
    lane, core = col_place // 2, lax.rem(col_place, 2)
    row_ring = Ring("row", [ring_of_rows(rows)], row_place)
    row_order = jnp.array(ring_of_rows(rows), jnp.int32)
    lane_ring = Ring("col", [[i * 2 + c for i in range(lanes)] for c in range(2)], col_place)
    swap = [(i, i ^ 1) for i in range(cols)]

    def other_core(block):
        return lax.ppermute(block, "col", swap)

    tokens = segment_ids.shape[0]
    row_tokens, col_tokens = tokens // rows, tokens // cols
    part_tokens = tokens // PARTS
    row_part, col_part = row_tokens // PARTS, col_tokens // PARTS
    model_width = residual.shape[1] * rows
    row_width = residual.shape[1]
    query_cols, kv_cols = w_query.shape[1], w_key.shape[1]
    kv_local = kv_cols // HEAD_SIZE
    heads = query_cols // HEAD_SIZE
    group = heads // kv_local
    first_row = row_place * row_tokens

    def gather_cols(block):
        m, w = block.shape
        placed = [((lane_ring.at(i), 0, 0), b[None]) for i, b in lane_ring.all_gather(block)]
        mine = place_blocks((lanes, m, w), block.dtype, placed)
        theirs = other_core(mine)
        both = place_blocks(
            (lanes, 2, m, w),
            block.dtype,
            [((0, core, 0, 0), mine[:, None]), ((0, 1 - core, 0, 0), theirs[:, None])],
        )
        return both.reshape(cols * m, w)

    def scatter_cols(block):
        m, w = block.shape[0] // cols, block.shape[1]
        split = block.reshape(lanes, 2, m, w)
        got = other_core(lax.dynamic_slice(split, (0, 1 - core, 0, 0), (lanes, 1, m, w)))
        kept = lax.dynamic_slice(split, (0, core, 0, 0), (lanes, 1, m, w))
        summed = (kept.astype(jnp.float32) + got.astype(jnp.float32)).reshape(lanes, m, w)
        if lanes > 1:
            summed = summed.astype(jnp.bfloat16)
        return lane_ring.reduce_scatter(
            lambda i: lax.dynamic_slice(summed, (lane_ring.at(i), 0, 0), (1, m, w))[0]
        )

    def row_blocks(block):
        m, w = block.shape[0] // rows, block.shape[1]

        def take(i):
            return lax.dynamic_slice(block, (row_order[row_ring.at(i)] * m, 0), (m, w))

        return take

    def gather_rows(block, along):
        m, w = block.shape
        shape = (rows * m, w) if along == 0 else (m, rows * w)
        placed = []
        for i, b in row_ring.all_gather(block):
            who = row_order[row_ring.at(i)]
            placed.append(((who * m, 0) if along == 0 else (0, who * w), b))
        return place_blocks(shape, block.dtype, placed)

    query_index = first_row + jnp.arange(row_tokens, dtype=jnp.int32)
    own_segment = lax.dynamic_slice_in_dim(segment_ids, first_row, row_tokens, 0)
    seg_starts = jnp.sum((segment_ids[None, :] < own_segment[:, None]).astype(jnp.int32), axis=1)
    tables = rotary_tables(query_index - seg_starts)

    gathered = gather_cols(residual)
    widened = gathered.astype(jnp.float32)
    scaled = (widened * attn_gain[None, :]).astype(jnp.bfloat16)
    sums = jnp.sum(widened * widened, axis=1)
    bit = 1
    while bit < rows:
        sums = sums + lax.ppermute(sums, "row", [(i, i ^ bit) for i in range(rows)])
        bit *= 2
    attn_scale = lax.rsqrt(
        lax.dynamic_slice_in_dim(sums, first_row, row_tokens, 0) / model_width + EPSILON
    )[:, None]

    kv_terms = jnp.concatenate([dot32(scaled, w_key), dot32(scaled, value_weight)], axis=1)
    kv_own = row_ring.reduce_scatter(row_blocks(kv_terms.astype(jnp.bfloat16))) * attn_scale
    key_own = rotary_apply(kv_own[:, :kv_cols].reshape(row_tokens, kv_local, HEAD_SIZE), tables)
    key_value = jnp.concatenate([key_own.reshape(row_tokens, kv_cols), kv_own[:, kv_cols:]], axis=1)
    key_value = gather_rows(key_value.astype(jnp.bfloat16), 0)
    key_all, value_all = key_value[:, :kv_cols], key_value[:, kv_cols:]
    key_heads = key_all.reshape(tokens, kv_local, HEAD_SIZE)
    value_heads = value_all.reshape(tokens, kv_local, HEAD_SIZE)
    key_index = jnp.arange(tokens, dtype=jnp.int32)

    def attend(part):
        terms = dot32(scaled.reshape(rows, PARTS, row_part, row_width)[:, part].reshape(part_tokens, row_width), w_query)
        own = slice(part * row_part, (part + 1) * row_part)
        queries = row_ring.reduce_scatter(row_blocks(terms.astype(jnp.bfloat16))) * attn_scale[own]
        queries = rotary_apply(
            queries.reshape(row_part, heads, HEAD_SIZE), (tables[0][own], tables[1][own])
        ).astype(jnp.bfloat16)
        key_mask = (
            (segment_ids[None, :] == own_segment[own][:, None])
            & (key_index[None, :] <= query_index[own][:, None])
        )[None, None]
        scores = jnp.where(
            key_mask,
            jnp.einsum(
                "tjgd,sjd->jgts",
                queries.reshape(row_part, kv_local, group, HEAD_SIZE),
                key_heads,
                preferred_element_type=jnp.float32,
            )
            * HEAD_SIZE ** (-0.5),
            NEGATIVE,
        )
        peak_score = jnp.max(scores, axis=3, keepdims=True)
        weights = jnp.where(key_mask, jnp.exp(scores - peak_score), 0.0).astype(jnp.bfloat16)
        weight_sum = jnp.sum(weights.astype(jnp.float32), axis=3)
        mixture = jnp.einsum(
            "jgts,sjd->jgtd", weights, value_heads, preferred_element_type=jnp.float32
        )
        attended = (
            jnp.transpose(mixture / weight_sum[..., None], (2, 0, 1, 3))
            .reshape(row_part, query_cols)
            .astype(jnp.bfloat16)
        )
        return gather_rows(attended, 0)

    def project(part, attended):
        attn_out = scatter_cols(dot32(attended, w_out).astype(jnp.bfloat16))
        own = residual.reshape(rows // cols, PARTS, row_part, row_width)[:, part]
        own = own.reshape(col_part, row_width)
        hidden_stream = (own.astype(jnp.float32) + attn_out).astype(jnp.bfloat16)
        full_rows = gather_rows(hidden_stream, 1)
        full32 = full_rows.astype(jnp.float32)
        scale = lax.rsqrt(jnp.sum(full32 * full32, axis=1) / model_width + EPSILON)[:, None]
        m, w = col_part, model_width // cols
        span = 2 * w
        placed = [
            (
                (lane_ring.at(0), 0, 0),
                lax.dynamic_slice(full_rows, (0, lane * span), (m, span))[None],
            )
        ]
        for hop in range(1, lanes):
            pairs = [
                (i * 2 + c, ((i + hop) % lanes) * 2 + c) for i in range(lanes) for c in range(2)
            ]
            sent = lax.dynamic_slice(full_rows, (0, lane_ring.at(hop) * span), (m, span))
            placed.append(((lane_ring.at(-hop), 0, 0), lax.ppermute(sent, "col", pairs)[None]))
        mine = place_blocks((lanes, m, span), full_rows.dtype, placed)
        theirs = other_core(lax.dynamic_slice(mine, (0, 0, (1 - core) * w), (lanes, m, w)))
        kept = lax.dynamic_slice(mine, (0, 0, core * w), (lanes, m, w))
        stream = place_blocks(
            (lanes, 2, m, w),
            full_rows.dtype,
            [((0, core, 0, 0), kept[:, None]), ((0, 1 - core, 0, 0), theirs[:, None])],
        ).reshape(part_tokens, w)
        return stream, scale

    def feed(stream, scale):
        mid = (stream.astype(jnp.float32) * mlp_gain[None, :]).astype(jnp.bfloat16)
        gate = scatter_cols(dot32(mid, w_gate).astype(jnp.bfloat16)) * scale
        up = scatter_cols(dot32(mid, w_up).astype(jnp.bfloat16)) * scale
        hidden = (jax.nn.silu(gate) * up).astype(jnp.bfloat16)
        down = dot32(gather_cols(hidden), w_down).astype(jnp.bfloat16)
        mlp_out = row_ring.reduce_scatter(row_blocks(down))
        own = lax.dynamic_slice_in_dim(stream, row_place * row_part, row_part, 0)
        return (own.astype(jnp.float32) + mlp_out).astype(jnp.bfloat16)

    outs = []
    for part in range(PARTS):
        stream, scale = project(part, attend(part))
        outs.append(feed(stream, scale))
    output = jnp.concatenate(outs, axis=0)

    block_count = page_table.shape[0]
    page_size = tokens // block_count
    slots_local = block_count // rows
    slot_ids = row_place * slots_local + jnp.arange(slots_local, dtype=jnp.int32)
    block_ids = jnp.arange(block_count, dtype=jnp.int32)
    owned_blocks = jnp.sum(
        jnp.where(page_table[None, :] == slot_ids[:, None], block_ids[None, :], 0), axis=1
    )
    page_rows = owned_blocks[:, None] * page_size + jnp.arange(page_size, dtype=jnp.int32)[None, :]
    key_cache_pages = jnp.take(key_all, page_rows, axis=0)
    value_cache_pages = jnp.take(value_all, page_rows, axis=0)
    return (output, key_cache_pages, value_cache_pages)


def solution(mesh):
    return jax.shard_map(
        per_device,
        mesh=mesh,
        in_specs=(
            P("col", "row"),
            P("row"),
            P("row", "col"),
            P("row", "col"),
            P("row", "col"),
            P("col", "row"),
            P("col"),
            P("col", "row"),
            P("col", "row"),
            P("row", "col"),
            P(),
            P(),
        ),
        out_specs=(P("row", "col"), P("row", None, "col"), P("row", None, "col")),
        check_vma=False,
    )
```

```python
import jax
import jax.numpy as jnp
from jax import lax
from jax.sharding import PartitionSpec as P

HEAD_SIZE = 128
ROPE_BASE = 5000000.0
EPSILON = 1e-05
NEGATIVE = -1e30
PARTS = 2


def quotient(value, size):
    if size & (size - 1):
        return lax.div(value, jnp.int32(size))
    return lax.shift_right_logical(value, jnp.int32(size.bit_length() - 1)) if size > 1 else value


def remainder(value, size):
    if size & (size - 1):
        return lax.rem(value, jnp.int32(size))
    return jnp.bitwise_and(value, jnp.int32(size - 1))


def cut_from(block, start, sizes):
    return lax.dynamic_slice(block, start, sizes, allow_negative_indices=False)


class RowWalk:
    def __init__(self, rows):
        self.depth = 4 if rows % 4 == 0 else 1
        self.width = rows // self.depth
        self.rows = rows

    def turned(self, x, z):
        if self.depth & (self.depth - 1) == 0 and self.width == 2:
            return jnp.bitwise_xor(z, x * (self.depth - 1))
        return jnp.where(remainder(x, 2) == 1, self.depth - 1 - z, z)

    def row_at(self, spot):
        x = quotient(spot, self.depth)
        return self.turned(x, remainder(spot, self.depth)) * self.width + x

    def spot_of(self, row):
        x = remainder(row, self.width)
        return x * self.depth + self.turned(x, quotient(row, self.width))

    def listed(self):
        walk = []
        for x in range(self.width):
            zs = range(self.depth) if x % 2 == 0 else reversed(range(self.depth))
            walk += [z * self.width + x for z in zs]
        return walk


class Ring:
    def __init__(self, axis, walks, spot):
        self.axis = axis
        self.size = n = len(walks[0])
        self.right = [(w[i], w[(i + 1) % n]) for w in walks for i in range(n)]
        self.left = [(w[(i + 1) % n], w[i]) for w in walks for i in range(n)]
        self.spot = spot

    def send(self, block, pairs):
        return lax.ppermute(block, self.axis, pairs)

    def at(self, offset):
        return remainder(self.spot + offset % self.size, self.size) if offset % self.size else self.spot

    def reduce_scatter(self, take):
        n, half = self.size, self.size // 2
        if n == 1:
            return take(0).astype(jnp.float32)
        if n == 2:
            got = self.send(take(1).astype(jnp.bfloat16), self.right)
            return take(0).astype(jnp.float32) + got.astype(jnp.float32)
        far = take(half).astype(jnp.bfloat16)
        cut = far.shape[0] // 2
        going_right = self.send(far[:cut], self.right).astype(jnp.float32)
        going_left = self.send(far[cut:], self.left).astype(jnp.float32)
        for step in range(half - 1, 0, -1):
            one = take(step).astype(jnp.float32)
            two = take(-step).astype(jnp.float32)
            if step == half - 1:
                one = jnp.concatenate([one[:cut] + going_right, one[cut:]], axis=0)
                two = jnp.concatenate([two[:cut], two[cut:] + going_left], axis=0)
            else:
                one = one + going_right
                two = two + going_left
            going_right = self.send(one.astype(jnp.bfloat16), self.right).astype(jnp.float32)
            going_left = self.send(two.astype(jnp.bfloat16), self.left).astype(jnp.float32)
        return take(0).astype(jnp.float32) + going_right + going_left

    def all_gather(self, block):
        n, half = self.size, self.size // 2
        if n == 1:
            return [(0, block)]
        if n == 2:
            return [(0, block), (1, self.send(block, self.right))]
        found = [(0, block)]
        from_left = from_right = block
        for step in range(1, half):
            from_left = self.send(from_left, self.right)
            from_right = self.send(from_right, self.left)
            found += [(-step, from_left), (step, from_right)]
        cut = block.shape[0] // 2
        far = jnp.concatenate(
            [self.send(from_left[:cut], self.right), self.send(from_right[cut:], self.left)], axis=0
        )
        return found + [(half, far)]


def place_blocks(shape, dtype, placed):
    buffer = jnp.zeros(shape, dtype)
    for start, block in placed:
        buffer = lax.dynamic_update_slice(buffer, block, start, allow_negative_indices=False)
    return buffer


def tie(block, *earlier):
    return lax.optimization_barrier((block, *earlier))[0]


def rotary_tables(token_positions):
    half_width = HEAD_SIZE // 2
    frequency = ROPE_BASE ** (-2.0 * jnp.arange(half_width, dtype=jnp.float32) / HEAD_SIZE)
    angles = token_positions.astype(jnp.float32)[:, None] * frequency[None, :]
    return jnp.cos(angles)[:, None, :], jnp.sin(angles)[:, None, :]


def rotary_apply(block, tables):
    cosine, sine_part = tables
    half_width = block.shape[-1] // 2
    first_half = block[..., :half_width]
    second = block[..., half_width:]
    return jnp.concatenate(
        [first_half * cosine - second * sine_part, second * cosine + first_half * sine_part],
        axis=-1,
    )


def dot32(a, b):
    return jnp.dot(a, b, preferred_element_type=jnp.float32)


def per_device(
    residual,
    attn_gain,
    w_query,
    w_key,
    value_weight,
    w_out,
    mlp_gain,
    w_gate,
    w_up,
    w_down,
    segment_ids,
    page_table,
):
    rows, cols = lax.axis_size("row"), lax.axis_size("col")
    row_place, col_place = lax.axis_index("row"), lax.axis_index("col")
    lanes = cols // 2
    lane, core = quotient(col_place, 2), remainder(col_place, 2)
    walk = RowWalk(rows)
    row_ring = Ring("row", [walk.listed()], walk.spot_of(row_place))
    lane_ring = Ring("col", [[i * 2 + c for i in range(lanes)] for c in range(2)], lane)
    row_at = [row_place] + [walk.row_at(row_ring.at(i)) for i in range(1, rows)]
    swap = [(i, i ^ 1) for i in range(cols)]

    def other_core(block):
        return lax.ppermute(block, "col", swap)

    tokens = segment_ids.shape[0]
    row_tokens, col_tokens = tokens // rows, tokens // cols
    part_tokens = tokens // PARTS
    row_part, col_part = row_tokens // PARTS, col_tokens // PARTS
    per_col = rows // cols
    row_width = residual.shape[1]
    model_width = row_width * rows
    query_cols, kv_cols = w_query.shape[1], w_key.shape[1]
    kv_local = kv_cols // HEAD_SIZE
    heads = query_cols // HEAD_SIZE
    group = heads // kv_local
    first_row = row_place * row_tokens

    def slot_of_row(who, m):
        if lanes <= 2 and per_col & (per_col - 1) == 0:
            return jnp.bitwise_xor(who, col_place * per_col) * m
        at_col = quotient(who, per_col)
        step = remainder(quotient(at_col, 2) - lane + lanes, lanes)
        side = jnp.bitwise_xor(remainder(at_col, 2), core)
        return ((step * 2 + side) * per_col + remainder(who, per_col)) * m

    def gather_cols(block, send_after=()):
        near = other_core(block)
        found = sorted(lane_ring.all_gather(tie(block, *send_after) if send_after else block), key=lambda f: f[0] % lanes)
        pieces = [block, near]
        for _, b in found[1:]:
            pieces += [b, other_core(b)]
        return jnp.concatenate(pieces, axis=0), found[-1][1]

    def core_sum(block):
        m, w = block.shape[0] // cols, block.shape[1]
        split = block.reshape(lanes, 2, m, w)
        got = other_core(split[:, 1])
        return (split[:, 0].astype(jnp.float32) + got.astype(jnp.float32)).astype(jnp.bfloat16)

    def lane_sum(summed):
        return lane_ring.reduce_scatter(lambda i: summed[i % lanes])

    def row_blocks(block, m):
        def take(i):
            start = slot_of_row(row_at[i], m)
            return cut_from(block, (start, 0), (m, block.shape[1]))

        return take

    def gather_rows(block, along, start_of, first_after=()):
        m, w = block.shape
        shape = (rows * m, w) if along == 0 else (m, rows * w)
        placed = []
        found = row_ring.all_gather(tie(block, *first_after) if first_after else block)
        for i, b in found:
            begin = start_of(row_at[i])
            placed.append(((begin, 0) if along == 0 else (0, begin), b))
        late = tuple(b for _, b in found[-3:-1])
        return place_blocks(shape, block.dtype, placed), late

    gathered, _ = gather_cols(residual)
    widened = gathered.astype(jnp.float32)
    scaled = (widened * attn_gain[None, :]).astype(jnp.bfloat16)
    sums = jnp.sum(widened * widened, axis=1)

    kv_terms = jnp.concatenate([dot32(scaled, w_key), dot32(scaled, value_weight)], axis=1)
    kv_terms = kv_terms.astype(jnp.bfloat16)

    late_ids, late_pages, sums = lax.optimization_barrier((segment_ids, page_table, sums, kv_terms))[:3]
    query_index = first_row + jnp.arange(row_tokens, dtype=jnp.int32)
    own_segment = cut_from(late_ids, (first_row,), (row_tokens,))
    seg_starts = jnp.sum((late_ids[None, :] < own_segment[:, None]).astype(jnp.int32), axis=1)
    tables = rotary_tables(query_index - seg_starts)
    key_rows = walk.row_at(remainder(row_ring.spot + jnp.arange(rows, dtype=jnp.int32), rows))
    key_index = key_rows[:, None] * row_tokens + jnp.arange(row_tokens, dtype=jnp.int32)[None, :]
    key_index = key_index.reshape(tokens)
    key_segment = jnp.sum(
        jnp.where(
            key_rows[:, None, None] == jnp.arange(rows, dtype=jnp.int32)[None, :, None],
            late_ids.reshape(1, rows, row_tokens),
            0,
        ),
        axis=1,
    ).reshape(tokens)
    bit = 1
    while bit < rows:
        sums = sums + lax.ppermute(sums, "row", [(i, i ^ bit) for i in range(rows)])
        bit *= 2
    attn_scale = lax.rsqrt(
        cut_from(sums, (slot_of_row(row_place, row_tokens),), (row_tokens,)) / model_width
        + EPSILON
    )[:, None]

    query_terms = dot32(scaled, w_query).astype(jnp.bfloat16)
    kv_own = row_ring.reduce_scatter(row_blocks(kv_terms, row_tokens)) * attn_scale
    key_own = rotary_apply(kv_own[:, :kv_cols].reshape(row_tokens, kv_local, HEAD_SIZE), tables)
    key_value = jnp.concatenate([key_own.reshape(row_tokens, kv_cols), kv_own[:, kv_cols:]], axis=1)
    found = row_ring.all_gather(key_value.astype(jnp.bfloat16))
    key_value = jnp.concatenate([b for _, b in sorted(found, key=lambda f: f[0] % rows)], axis=0)
    key_all, value_all = key_value[:, :kv_cols], key_value[:, kv_cols:]
    key_heads = key_all.reshape(tokens, kv_local, HEAD_SIZE)
    value_heads = value_all.reshape(tokens, kv_local, HEAD_SIZE)

    queries = row_ring.reduce_scatter(row_blocks(query_terms, row_tokens)) * attn_scale
    queries = rotary_apply(queries.reshape(row_tokens, heads, HEAD_SIZE), tables)
    queries = queries.astype(jnp.bfloat16)

    def attend(part):
        own = slice(part * row_part, (part + 1) * row_part)
        key_mask = (
            (key_segment[None, :] == own_segment[own][:, None])
            & (key_index[None, :] <= query_index[own][:, None])
        )[None, None]
        scores = jnp.where(
            key_mask,
            jnp.einsum(
                "tjgd,sjd->jgts",
                queries[own].reshape(row_part, kv_local, group, HEAD_SIZE),
                key_heads,
                preferred_element_type=jnp.float32,
            )
            * HEAD_SIZE ** (-0.5),
            NEGATIVE,
        )
        peak_score = jnp.max(scores, axis=3, keepdims=True)
        weights = jnp.where(key_mask, jnp.exp(scores - peak_score), 0.0).astype(jnp.bfloat16)
        weight_sum = jnp.sum(weights.astype(jnp.float32), axis=3)
        mixture = jnp.einsum(
            "jgts,sjd->jgtd", weights, value_heads, preferred_element_type=jnp.float32
        )
        return (
            jnp.transpose(mixture / weight_sum[..., None], (2, 0, 1, 3))
            .reshape(row_part, query_cols)
            .astype(jnp.bfloat16)
        )

    def project(part, attended):
        attn_out = lane_sum(core_sum(dot32(attended, w_out).astype(jnp.bfloat16)))
        own = residual.reshape(per_col, PARTS, row_part, row_width)[:, part]
        own = own.reshape(col_part, row_width)
        return (own.astype(jnp.float32) + attn_out).astype(jnp.bfloat16)

    def spread(full_rows, before_core=()):
        w = model_width // cols
        span = 2 * w
        mine = [(0, cut_from(full_rows, (0, lane * span), (col_part, span)))]
        for hop in range(1, lanes):
            pairs = [
                (i * 2 + c, ((i + hop) % lanes) * 2 + c) for i in range(lanes) for c in range(2)
            ]
            sent = cut_from(full_rows, (0, lane_ring.at(hop) * span), (col_part, span))
            mine.append((-hop % lanes, lax.ppermute(sent, "col", pairs)))
        pieces = []
        for hop, b in sorted(mine, key=lambda f: f[0]):
            sent = cut_from(b, (0, (1 - core) * w), (col_part, w))
            if hop and before_core:
                sent = tie(sent, *before_core)
            pieces += [cut_from(b, (0, core * w), (col_part, w)), other_core(sent)]
        return jnp.concatenate(pieces, axis=0)

    def mlp_scale(full_rows):
        full32 = full_rows.astype(jnp.float32)
        return lax.rsqrt(jnp.sum(full32 * full32, axis=1) / model_width + EPSILON)[:, None]

    def widen(stream):
        mid = (stream.astype(jnp.float32) * mlp_gain[None, :]).astype(jnp.bfloat16)
        return (
            core_sum(dot32(mid, w_gate).astype(jnp.bfloat16)),
            core_sum(dot32(mid, w_up).astype(jnp.bfloat16)),
        )

    def finish(hidden_all, stream):
        down = dot32(hidden_all, w_down).astype(jnp.bfloat16)
        mlp_out = row_ring.reduce_scatter(row_blocks(down, row_part))
        own = cut_from(stream, (slot_of_row(row_place, row_part), 0), (row_part, stream.shape[1]))
        return (own.astype(jnp.float32) + mlp_out).astype(jnp.bfloat16)

    def part_slot(who):
        return slot_of_row(who, row_part)

    parts = range(PARTS)
    attended, late = [], ()
    for part in parts:
        got, late = gather_rows(attend(part), 0, part_slot, late)
        attended.append(got)
    full, late = [], ()
    for part in parts:
        got, late = gather_rows(project(part, attended[part]), 1, lambda who: who * row_width, late)
        full.append(got)
    streams, gates, ups, after = [], [], [], ()
    for part in parts:
        stream = spread(full[part], after)
        gate, up = widen(tie(stream, *after) if after else stream)
        streams.append(stream)
        gates.append(gate)
        ups.append(up)
        after = (gate, up)
    hidden, outs, after = [], [], ()
    for part in parts:
        scale = mlp_scale(full[part])
        gate = lane_sum(gates[part]) * scale
        up = lane_sum(tie(ups[part], *after) if after else ups[part]) * scale
        own = (jax.nn.silu(gate) * up).astype(jnp.bfloat16)
        everyone, far = gather_cols(own)
        after = (far,)
        outs.append(finish(everyone, streams[part]))
    output = jnp.concatenate(outs, axis=0)

    block_count = page_table.shape[0]
    page_size = tokens // block_count
    slots_local = block_count // rows
    slot_ids = row_place * slots_local + jnp.arange(slots_local, dtype=jnp.int32)
    block_ids = jnp.arange(block_count, dtype=jnp.int32)
    owned_blocks = jnp.sum(
        jnp.where(late_pages[None, :] == slot_ids[:, None], block_ids[None, :], 0), axis=1
    )
    row_blocks_count = block_count // rows
    at_row = quotient(owned_blocks, row_blocks_count)
    away = remainder(walk.spot_of(at_row) - row_ring.spot + rows, rows)
    owned_blocks = away * row_blocks_count + remainder(owned_blocks, row_blocks_count)
    page_rows = owned_blocks[:, None] * page_size + jnp.arange(page_size, dtype=jnp.int32)[None, :]
    key_cache_pages = jnp.take(key_all, page_rows, axis=0)
    value_cache_pages = jnp.take(value_all, page_rows, axis=0)
    return (output, key_cache_pages, value_cache_pages)


def solution(mesh):
    return jax.shard_map(
        per_device,
        mesh=mesh,
        in_specs=(
            P("col", "row"),
            P("row"),
            P("row", "col"),
            P("row", "col"),
            P("row", "col"),
            P("col", "row"),
            P("col"),
            P("col", "row"),
            P("col", "row"),
            P("row", "col"),
            P(),
            P(),
        ),
        out_specs=(P("row", "col"), P("row", None, "col"), P("row", None, "col")),
        check_vma=False,
    )
```

```python
import jax
import jax.numpy as jnp
from jax import lax
from jax.sharding import PartitionSpec as P

HEAD_SIZE = 128
ROPE_BASE = 5000000.0
EPSILON = 1e-05
NEGATIVE = -1e30
PARTS = 2
LAST = 3
LAG = 2


def quotient(value, size):
    if size & (size - 1):
        return lax.div(value, jnp.int32(size))
    return lax.shift_right_logical(value, jnp.int32(size.bit_length() - 1)) if size > 1 else value


def remainder(value, size):
    if size & (size - 1):
        return lax.rem(value, jnp.int32(size))
    return jnp.bitwise_and(value, jnp.int32(size - 1))


def cut_from(block, start, sizes):
    return lax.dynamic_slice(block, start, sizes, allow_negative_indices=False)


class RowWalk:
    def __init__(self, rows):
        self.depth = 4 if rows % 4 == 0 else 1
        self.width = rows // self.depth
        self.rows = rows

    def turned(self, x, z):
        if self.depth & (self.depth - 1) == 0 and self.width == 2:
            return jnp.bitwise_xor(z, x * (self.depth - 1))
        return jnp.where(remainder(x, 2) == 1, self.depth - 1 - z, z)

    def row_at(self, spot):
        x = quotient(spot, self.depth)
        return self.turned(x, remainder(spot, self.depth)) * self.width + x

    def spot_of(self, row):
        x = remainder(row, self.width)
        return x * self.depth + self.turned(x, quotient(row, self.width))

    def listed(self):
        walk = []
        for x in range(self.width):
            zs = range(self.depth) if x % 2 == 0 else reversed(range(self.depth))
            walk += [z * self.width + x for z in zs]
        return walk


class Ring:
    def __init__(self, axis, walks, spot):
        self.axis = axis
        self.size = n = len(walks[0])
        self.right = [(w[i], w[(i + 1) % n]) for w in walks for i in range(n)]
        self.left = [(w[(i + 1) % n], w[i]) for w in walks for i in range(n)]
        self.spot = spot

    def send(self, block, pairs):
        return lax.ppermute(block, self.axis, pairs)

    def at(self, offset):
        return remainder(self.spot + offset % self.size, self.size) if offset % self.size else self.spot

    def reduce_scatter(self, take):
        return SumWalk(self, take).run()

    def all_gather(self, block):
        return GatherWalk(self, block).run()


class SumWalk:
    def __init__(self, ring, take):
        self.ring, self.take, self.done = ring, take, 0
        self.steps = ring.size // 2
        self.sent = self.got = ()

    def step(self, after=()):
        ring, take, half = self.ring, self.take, self.steps
        self.done += 1
        if ring.size == 2:
            right, left = take(1).astype(jnp.bfloat16), None
        elif self.done == 1:
            far = take(half).astype(jnp.bfloat16)
            self.cut = far.shape[0] // 2
            right, left = far[: self.cut], far[self.cut :]
        else:
            place = half - self.done + 1
            right = take(place).astype(jnp.float32)
            left = take(-place).astype(jnp.float32)
            going_right, going_left = (g.astype(jnp.float32) for g in self.got)
            if self.done == 2:
                cut = self.cut
                right = jnp.concatenate([right[:cut] + going_right, right[cut:]], axis=0)
                left = jnp.concatenate([left[:cut], left[cut:] + going_left], axis=0)
            else:
                right, left = right + going_right, left + going_left
            right, left = right.astype(jnp.bfloat16), left.astype(jnp.bfloat16)
        if left is None:
            self.sent = (tie(right, *after),)
            self.got = (ring.send(self.sent[0], ring.right),)
        else:
            self.sent = tie_all((right, left), after)
            self.got = (ring.send(self.sent[0], ring.right), ring.send(self.sent[1], ring.left))

    def result(self):
        total = self.take(0).astype(jnp.float32)
        for block in self.got:
            total = total + block.astype(jnp.float32)
        return total

    def run(self):
        while self.done < self.steps:
            self.step()
        return self.result()


class GatherWalk:
    def __init__(self, ring, block):
        self.ring, self.done = ring, 0
        self.steps = ring.size // 2
        self.found = [(0, block)]
        self.got = (block, block)

    def step(self, after=()):
        ring = self.ring
        self.done += 1
        if ring.size == 2:
            self.got = (ring.send(tie(self.got[0], *after), ring.right),)
            self.found.append((1, self.got[0]))
            return
        right, left = tie_all(self.got, after)
        if self.done == self.steps:
            cut = right.shape[0] // 2
            right, left = right[:cut], left[cut:]
        self.got = (ring.send(right, ring.right), ring.send(left, ring.left))
        if self.done == self.steps:
            self.found.append((self.done, jnp.concatenate(self.got, axis=0)))
        else:
            self.found += [(-self.done, self.got[0]), (self.done, self.got[1])]

    def run(self):
        while self.done < self.steps:
            self.step()
        return self.found


def tie_all(blocks, earlier):
    if len(blocks) + len(earlier) < 2:
        return tuple(blocks)
    return tuple(lax.optimization_barrier((*blocks, *earlier))[: len(blocks)])


def tie(block, *earlier):
    return tie_all((block,), earlier)[0]


def place_blocks(shape, dtype, placed):
    buffer = jnp.zeros(shape, dtype)
    for start, block in placed:
        buffer = lax.dynamic_update_slice(buffer, block, start, allow_negative_indices=False)
    return buffer


def rotary_tables(token_positions):
    half_width = HEAD_SIZE // 2
    frequency = ROPE_BASE ** (-2.0 * jnp.arange(half_width, dtype=jnp.float32) / HEAD_SIZE)
    angles = token_positions.astype(jnp.float32)[:, None] * frequency[None, :]
    return jnp.cos(angles)[:, None, :], jnp.sin(angles)[:, None, :]


def rotary_apply(block, tables):
    cosine, sine_part = tables
    half_width = block.shape[-1] // 2
    first_half = block[..., :half_width]
    second = block[..., half_width:]
    return jnp.concatenate(
        [first_half * cosine - second * sine_part, second * cosine + first_half * sine_part],
        axis=-1,
    )


def dot32(a, b):
    return jnp.dot(a, b, preferred_element_type=jnp.float32)


def per_device(
    residual,
    attn_gain,
    w_query,
    w_key,
    value_weight,
    w_out,
    mlp_gain,
    w_gate,
    w_up,
    w_down,
    segment_ids,
    page_table,
):
    rows, cols = lax.axis_size("row"), lax.axis_size("col")
    row_place, col_place = lax.axis_index("row"), lax.axis_index("col")
    lanes = cols // 2
    lane, core = quotient(col_place, 2), remainder(col_place, 2)
    walk = RowWalk(rows)
    row_ring = Ring("row", [walk.listed()], walk.spot_of(row_place))
    lane_ring = Ring("col", [[i * 2 + c for i in range(lanes)] for c in range(2)], lane)
    row_at = [row_place] + [walk.row_at(row_ring.at(i)) for i in range(1, rows)]
    swap = [(i, i ^ 1) for i in range(cols)]

    def other_core(block):
        return lax.ppermute(block, "col", swap)

    tokens = segment_ids.shape[0]
    row_tokens, col_tokens = tokens // rows, tokens // cols
    part_tokens = tokens // PARTS
    row_part, col_part = row_tokens // PARTS, col_tokens // PARTS
    per_col = rows // cols
    row_width = residual.shape[1]
    model_width = row_width * rows
    query_cols, kv_cols = w_query.shape[1], w_key.shape[1]
    kv_local = kv_cols // HEAD_SIZE
    heads = query_cols // HEAD_SIZE
    group = heads // kv_local
    first_row = row_place * row_tokens

    def slot_of_row(who, m):
        if lanes <= 2 and per_col & (per_col - 1) == 0:
            return jnp.bitwise_xor(who, col_place * per_col) * m
        at_col = quotient(who, per_col)
        step = remainder(quotient(at_col, 2) - lane + lanes, lanes)
        side = jnp.bitwise_xor(remainder(at_col, 2), core)
        return ((step * 2 + side) * per_col + remainder(who, per_col)) * m

    def gather_cols(block, after=()):
        near = other_core(block)
        found = sorted(lane_ring.all_gather(block), key=lambda f: f[0] % lanes)
        pieces = [block, near]
        for _, b in found[1:]:
            b = tie(b, *after)
            pieces += [b, other_core(b)]
        return jnp.concatenate(pieces, axis=0), found[-1][1]

    def core_sum(block):
        m, w = block.shape[0] // cols, block.shape[1]
        split = block.reshape(lanes, 2, m, w)
        got = other_core(split[:, 1])
        return (split[:, 0].astype(jnp.float32) + got.astype(jnp.float32)).astype(jnp.bfloat16)

    def lane_walk(summed):
        walk_on = SumWalk(lane_ring, lambda i: summed[i % lanes])
        while walk_on.done < walk_on.steps:
            walk_on.step()
        return walk_on

    def row_blocks(block, m):
        def take(i):
            start = slot_of_row(row_at[i], m)
            return cut_from(block, (start, 0), (m, block.shape[1]))

        return take

    def lay_out(found, along, start_of):
        m, w = found[0][1].shape
        shape = (rows * m, w) if along == 0 else (m, rows * w)
        placed = []
        for i, b in found:
            begin = start_of(row_at[i])
            placed.append(((begin, 0) if along == 0 else (0, begin), b))
        return place_blocks(shape, found[0][1].dtype, placed)

    gathered, _ = gather_cols(residual)
    widened = gathered.astype(jnp.float32)
    scaled = (widened * attn_gain[None, :]).astype(jnp.bfloat16)
    sums = jnp.sum(widened * widened, axis=1)

    kv_terms = jnp.concatenate([dot32(scaled, w_key), dot32(scaled, value_weight)], axis=1)
    kv_terms = kv_terms.astype(jnp.bfloat16)

    late_ids, late_pages, sums = lax.optimization_barrier((segment_ids, page_table, sums, kv_terms))[:3]
    query_index = first_row + jnp.arange(row_tokens, dtype=jnp.int32)
    own_segment = cut_from(late_ids, (first_row,), (row_tokens,))
    seg_starts = jnp.sum((late_ids[None, :] < own_segment[:, None]).astype(jnp.int32), axis=1)
    tables = rotary_tables(query_index - seg_starts)
    key_rows = walk.row_at(remainder(row_ring.spot + jnp.arange(rows, dtype=jnp.int32), rows))
    key_index = key_rows[:, None] * row_tokens + jnp.arange(row_tokens, dtype=jnp.int32)[None, :]
    key_index = key_index.reshape(tokens)
    key_segment = jnp.sum(
        jnp.where(
            key_rows[:, None, None] == jnp.arange(rows, dtype=jnp.int32)[None, :, None],
            late_ids.reshape(1, rows, row_tokens),
            0,
        ),
        axis=1,
    ).reshape(tokens)
    query_terms = dot32(tie(scaled, kv_terms), w_query).astype(jnp.bfloat16)
    query_walk = SumWalk(row_ring, row_blocks(query_terms, row_tokens))
    kv_walk = SumWalk(row_ring, row_blocks(kv_terms, row_tokens))
    kv_spread, bit = None, 1
    for step in range(query_walk.steps):
        query_walk.step()
        for turn in range(2):
            after = query_walk.sent if step and not turn else ()
            if kv_walk.done < kv_walk.steps:
                kv_walk.step(after)
                if bit < rows:
                    got = lax.ppermute(sums, "row", [(i, i ^ bit) for i in range(rows)])
                    sums = sums + tie(got, *kv_walk.got)
                    bit *= 2
                continue
            if kv_spread is None:
                attn_scale = lax.rsqrt(
                    cut_from(sums, (slot_of_row(row_place, row_tokens),), (row_tokens,)) / model_width
                    + EPSILON
                )[:, None]
                kv_own = kv_walk.result() * attn_scale
                key_own = rotary_apply(
                    kv_own[:, :kv_cols].reshape(row_tokens, kv_local, HEAD_SIZE), tables
                ).reshape(row_tokens, kv_cols)
                key_value = jnp.concatenate([key_own, kv_own[:, kv_cols:]], axis=1)
                kv_spread = GatherWalk(row_ring, key_value.astype(jnp.bfloat16))
            kv_spread.step(after)
    found = sorted(kv_spread.run(), key=lambda f: f[0] % rows)
    key_value = jnp.concatenate([b for _, b in found], axis=0)
    key_all, value_all = key_value[:, :kv_cols], key_value[:, kv_cols:]
    key_heads = key_all.reshape(tokens, kv_local, HEAD_SIZE)
    value_heads = value_all.reshape(tokens, kv_local, HEAD_SIZE)

    queries = query_walk.result() * attn_scale
    queries = rotary_apply(queries.reshape(row_tokens, heads, HEAD_SIZE), tables)
    queries = queries.astype(jnp.bfloat16)

    def attend(part, after=()):
        own = slice(part * row_part, (part + 1) * row_part)
        key_mask = (
            (key_segment[None, :] == own_segment[own][:, None])
            & (key_index[None, :] <= query_index[own][:, None])
        )[None, None]
        scores = jnp.where(
            key_mask,
            jnp.einsum(
                "tjgd,sjd->jgts",
                tie(queries[own], *after).reshape(row_part, kv_local, group, HEAD_SIZE),
                key_heads,
                preferred_element_type=jnp.float32,
            )
            * HEAD_SIZE ** (-0.5),
            NEGATIVE,
        )
        peak_score = jnp.max(scores, axis=3, keepdims=True)
        weights = jnp.where(key_mask, jnp.exp(scores - peak_score), 0.0).astype(jnp.bfloat16)
        weight_sum = jnp.sum(weights.astype(jnp.float32), axis=3)
        mixture = jnp.einsum(
            "jgts,sjd->jgtd", weights, value_heads, preferred_element_type=jnp.float32
        )
        return (
            jnp.transpose(mixture / weight_sum[..., None], (2, 0, 1, 3))
            .reshape(row_part, query_cols)
            .astype(jnp.bfloat16)
        )

    def head_sums(walk_on):
        attended = lay_out(walk_on.found, 0, lambda who: slot_of_row(who, row_part))
        return core_sum(dot32(attended, w_out).astype(jnp.bfloat16))

    def add_stream(part, summed):
        own = residual.reshape(per_col, PARTS, row_part, row_width)[:, part]
        own = own.reshape(col_part, row_width).astype(jnp.float32)
        return GatherWalk(row_ring, (own + lane_walk(summed).result()).astype(jnp.bfloat16))

    def spread(full_rows):
        w = model_width // cols
        span = 2 * w
        mine = [(0, cut_from(full_rows, (0, lane * span), (col_part, span)))]
        for hop in range(1, lanes):
            pairs = [
                (i * 2 + c, ((i + hop) % lanes) * 2 + c) for i in range(lanes) for c in range(2)
            ]
            sent = cut_from(full_rows, (0, lane_ring.at(hop) * span), (col_part, span))
            mine.append((-hop % lanes, lax.ppermute(sent, "col", pairs)))
        return [b for _, b in sorted(mine, key=lambda f: f[0])]

    def scale_of(blocks):
        total = 0.0
        for block in blocks:
            block = block.astype(jnp.float32)
            total = total + jnp.sum(block * block, axis=1)
        return lax.rsqrt(total / model_width + EPSILON)[:, None]

    def along_z(block, last_after):
        up = [(z * 2 + x, (z + 1) % 4 * 2 + x) for z in range(4) for x in range(2)]
        blocks = [block]
        while len(blocks) < 4:
            after = last_after if len(blocks) == LAST else ()
            blocks.append(lax.ppermute(tie(blocks[-1], *after), "row", up))
        return blocks

    def to_takers(blocks):
        z = quotient(row_place, 2)
        here = [quotient(remainder(z - i + 4, 4), 2) == lane for i in range(2)]
        given = [jnp.where(here[i], blocks[i + 2], blocks[i]) for i in range(2)]
        kept = [jnp.where(here[i], blocks[i], blocks[i + 2]) for i in range(2)]
        over = lax.ppermute(jnp.concatenate(given, axis=0), "col", [(i, i ^ 2) for i in range(cols)])
        came = [over[:col_part], over[col_part:]]
        first = remainder(jnp.bitwise_xor(z, core), 2) == 0
        mine = [jnp.where(first, b[0], b[1]) for b in (kept, came)]
        theirs = [jnp.where(first, b[1], b[0]) for b in (kept, came)]
        near = other_core(jnp.concatenate(theirs, axis=0))
        return jnp.concatenate([mine[0], near[:col_part], mine[1], near[col_part:]], axis=0)

    def join_x(own, other):
        x = remainder(row_place, 2)
        return jnp.concatenate(
            [jnp.where(x == 0, own, other), jnp.where(x == 0, other, own)], axis=1
        )

    def join_cores(mine, before_core):
        w = model_width // cols
        pieces = []
        for hop, b in enumerate(mine):
            if hop:
                b = tie(b, *before_core)
            sent = cut_from(b, (0, (1 - core) * w), (col_part, w))
            pieces += [cut_from(b, (0, core * w), (col_part, w)), other_core(sent)]
        return jnp.concatenate(pieces, axis=0)

    def widen(stream):
        mid = (stream.astype(jnp.float32) * mlp_gain[None, :]).astype(jnp.bfloat16)
        mid = lax.optimization_barrier(mid)
        gate = dot32(mid, w_gate).astype(jnp.bfloat16)
        up = dot32(mid, w_up).astype(jnp.bfloat16)
        return core_sum(gate), core_sum(up), (gate, up)

    block_0 = attend(0)
    heads_0 = GatherWalk(row_ring, block_0)
    heads_0.step()
    block_1 = attend(1, (block_0,))
    heads_1 = GatherWalk(row_ring, block_1)
    heads_0.step((block_1,))
    steps = heads_0.steps
    for step in range(2, steps):
        heads_0.step()
        heads_1.step(heads_0.found[-4][1:] if step == 2 else ())
    summed_0 = head_sums(heads_0)
    stream_0 = add_stream(0, summed_0)
    while heads_1.done < steps:
        heads_1.step((summed_0,) if heads_1.done == steps - 1 else ())
    stream_0.step()
    stream_0.step()
    second = stream_0.got
    full = lay_out(stream_0.run(), 1, lambda who: who * row_width)
    scales = [scale_of([full])]
    halves = spread(full)
    stream_1 = add_stream(1, head_sums(heads_1))
    if rows == 8 and cols == 4:
        swap_x = [(i, i ^ 1) for i in range(rows)]
        blocks = along_z(tie(stream_1.found[0][1], *second), halves[1:])
        total = 0.0
        for block in blocks:
            block = block.astype(jnp.float32)
            total = total + jnp.sum(block * block, axis=1)
        total = total + lax.ppermute(total, "row", swap_x)
        scales.append(lax.rsqrt(total / model_width + EPSILON)[:, None])
        own = to_takers(blocks)
        other = lax.ppermute(own, "row", swap_x)
        stream_0 = join_cores(halves, ())
        gate_0, up_0, terms_0 = widen(stream_0)
        stream_1 = join_x(own, tie(other, *terms_0))
    else:
        stream_1.step(second)
        full = lay_out(stream_1.run(), 1, lambda who: who * row_width)
        scales.append(scale_of([full]))
        stream_0 = join_cores(halves, ())
        gate_0, up_0, terms_0 = widen(stream_0)
        stream_1 = join_cores(spread(full), terms_0)

    def gated(gate, up, scale):
        return (jax.nn.silu(gate * scale) * (up * scale)).astype(jnp.bfloat16)

    def down_walk(everyone):
        down = dot32(everyone, w_down).astype(jnp.bfloat16)
        return SumWalk(row_ring, row_blocks(down, row_part))

    def finish(stream, walk_on):
        own = cut_from(stream, (slot_of_row(row_place, row_part), 0), (row_part, stream.shape[1]))
        return (own.astype(jnp.float32) + walk_on.result()).astype(jnp.bfloat16)

    gate_0, up_0 = lane_walk(gate_0), lane_walk(up_0)
    gate_1, up_1, terms_1 = widen(tie(stream_1, *gate_0.got))
    hidden_0 = gated(gate_0.result(), up_0.result(), scales[0])
    everyone, far = gather_cols(tie(hidden_0, *terms_1))
    gate_1, up_1 = lane_walk(tie(gate_1, far)), lane_walk(tie(up_1, far))
    down_0 = down_walk(everyone)
    while down_0.done < down_0.steps - 1:
        down_0.step()
    gate_1.got, up_1.got = tie_all(gate_1.got, down_0.got), tie_all(up_1.got, down_0.got)
    gate_1, up_1 = gate_1.result(), up_1.result()
    down_0.step()
    everyone, far = gather_cols(gated(gate_1, up_1, scales[1]), down_0.got)
    down_1 = down_walk(everyone)
    down_1.run()
    output = jnp.concatenate([finish(stream_0, down_0), finish(stream_1, down_1)], axis=0)

    block_count = page_table.shape[0]
    page_size = tokens // block_count
    slots_local = block_count // rows
    slot_ids = row_place * slots_local + jnp.arange(slots_local, dtype=jnp.int32)
    block_ids = jnp.arange(block_count, dtype=jnp.int32)
    owned_blocks = jnp.sum(
        jnp.where(late_pages[None, :] == slot_ids[:, None], block_ids[None, :], 0), axis=1
    )
    row_blocks_count = block_count // rows
    at_row = quotient(owned_blocks, row_blocks_count)
    away = remainder(walk.spot_of(at_row) - row_ring.spot + rows, rows)
    owned_blocks = away * row_blocks_count + remainder(owned_blocks, row_blocks_count)
    page_rows = owned_blocks[:, None] * page_size + jnp.arange(page_size, dtype=jnp.int32)[None, :]
    key_cache_pages = jnp.take(key_all, page_rows, axis=0)
    value_cache_pages = jnp.take(value_all, page_rows, axis=0)
    return (output, key_cache_pages, value_cache_pages)


def solution(mesh):
    return jax.shard_map(
        per_device,
        mesh=mesh,
        in_specs=(
            P("col", "row"),
            P("row"),
            P("row", "col"),
            P("row", "col"),
            P("row", "col"),
            P("col", "row"),
            P("col"),
            P("col", "row"),
            P("col", "row"),
            P("row", "col"),
            P(),
            P(),
        ),
        out_specs=(P("row", "col"), P("row", None, "col"), P("row", None, "col")),
        check_vma=False,
    )
```

```python
import jax
import jax.numpy as jnp
from jax import lax
from jax.sharding import PartitionSpec as P

HEAD_SIZE = 128
ROPE_BASE = 5000000.0
EPSILON = 1e-05
NEGATIVE = -1e30
PARTS = 2
LAST = 3
LAG = 2


def quotient(value, size):
    if size & (size - 1):
        return lax.div(value, jnp.int32(size))
    return lax.shift_right_logical(value, jnp.int32(size.bit_length() - 1)) if size > 1 else value


def remainder(value, size):
    if size & (size - 1):
        return lax.rem(value, jnp.int32(size))
    return jnp.bitwise_and(value, jnp.int32(size - 1))


def cut_from(block, start, sizes):
    return lax.dynamic_slice(block, start, sizes, allow_negative_indices=False)


class RowWalk:
    def __init__(self, rows):
        self.depth = 4 if rows % 4 == 0 else 1
        self.width = rows // self.depth
        self.rows = rows

    def turned(self, x, z):
        if self.depth & (self.depth - 1) == 0 and self.width == 2:
            return jnp.bitwise_xor(z, x * (self.depth - 1))
        return jnp.where(remainder(x, 2) == 1, self.depth - 1 - z, z)

    def row_at(self, spot):
        x = quotient(spot, self.depth)
        return self.turned(x, remainder(spot, self.depth)) * self.width + x

    def spot_of(self, row):
        x = remainder(row, self.width)
        return x * self.depth + self.turned(x, quotient(row, self.width))

    def listed(self):
        walk = []
        for x in range(self.width):
            zs = range(self.depth) if x % 2 == 0 else reversed(range(self.depth))
            walk += [z * self.width + x for z in zs]
        return walk


class Ring:
    def __init__(self, axis, walks, spot):
        self.axis = axis
        self.size = n = len(walks[0])
        self.right = [(w[i], w[(i + 1) % n]) for w in walks for i in range(n)]
        self.left = [(w[(i + 1) % n], w[i]) for w in walks for i in range(n)]
        self.spot = spot

    def send(self, block, pairs):
        return lax.ppermute(block, self.axis, pairs)

    def at(self, offset):
        return remainder(self.spot + offset % self.size, self.size) if offset % self.size else self.spot

    def reduce_scatter(self, take):
        return SumWalk(self, take).run()

    def all_gather(self, block):
        return GatherWalk(self, block).run()


class SumWalk:
    def __init__(self, ring, take):
        self.ring, self.take, self.done = ring, take, 0
        self.steps = ring.size // 2
        self.sent = self.got = ()

    def step(self, after=()):
        ring, take, half = self.ring, self.take, self.steps
        self.done += 1
        if ring.size == 2:
            right, left = take(1).astype(jnp.bfloat16), None
        elif self.done == 1:
            far = take(half).astype(jnp.bfloat16)
            self.cut = far.shape[0] // 2
            right, left = far[: self.cut], far[self.cut :]
        else:
            place = half - self.done + 1
            right = take(place).astype(jnp.float32)
            left = take(-place).astype(jnp.float32)
            going_right, going_left = (g.astype(jnp.float32) for g in self.got)
            if self.done == 2:
                cut = self.cut
                right = jnp.concatenate([right[:cut] + going_right, right[cut:]], axis=0)
                left = jnp.concatenate([left[:cut], left[cut:] + going_left], axis=0)
            else:
                right, left = right + going_right, left + going_left
            right, left = right.astype(jnp.bfloat16), left.astype(jnp.bfloat16)
        if left is None:
            self.sent = (tie(right, *after),)
            self.got = (ring.send(self.sent[0], ring.right),)
        else:
            self.sent = tie_all((right, left), after)
            self.got = (ring.send(self.sent[0], ring.right), ring.send(self.sent[1], ring.left))

    def result(self):
        total = self.take(0).astype(jnp.float32)
        for block in self.got:
            total = total + block.astype(jnp.float32)
        return total

    def run(self):
        while self.done < self.steps:
            self.step()
        return self.result()


class GatherWalk:
    def __init__(self, ring, block):
        self.ring, self.done = ring, 0
        self.steps = ring.size // 2
        self.found = [(0, block)]
        self.got = (block, block)

    def step(self, after=()):
        ring = self.ring
        self.done += 1
        if ring.size == 2:
            self.got = (ring.send(tie(self.got[0], *after), ring.right),)
            self.found.append((1, self.got[0]))
            return
        right, left = tie_all(self.got, after)
        if self.done == self.steps:
            cut = right.shape[0] // 2
            right, left = right[:cut], left[cut:]
        self.got = (ring.send(right, ring.right), ring.send(left, ring.left))
        if self.done == self.steps:
            self.found.append((self.done, jnp.concatenate(self.got, axis=0)))
        else:
            self.found += [(-self.done, self.got[0]), (self.done, self.got[1])]

    def run(self):
        while self.done < self.steps:
            self.step()
        return self.found


def tie_all(blocks, earlier):
    if len(blocks) + len(earlier) < 2:
        return tuple(blocks)
    return tuple(lax.optimization_barrier((*blocks, *earlier))[: len(blocks)])


def tie(block, *earlier):
    return tie_all((block,), earlier)[0]


def place_blocks(shape, dtype, placed):
    buffer = jnp.zeros(shape, dtype)
    for start, block in placed:
        buffer = lax.dynamic_update_slice(buffer, block, start, allow_negative_indices=False)
    return buffer


def rotary_tables(token_positions):
    half_width = HEAD_SIZE // 2
    frequency = ROPE_BASE ** (-2.0 * jnp.arange(half_width, dtype=jnp.float32) / HEAD_SIZE)
    angles = token_positions.astype(jnp.float32)[:, None] * frequency[None, :]
    return jnp.cos(angles)[:, None, :], jnp.sin(angles)[:, None, :]


def rotary_apply(block, tables):
    cosine, sine_part = tables
    half_width = block.shape[-1] // 2
    first_half = block[..., :half_width]
    second = block[..., half_width:]
    return jnp.concatenate(
        [first_half * cosine - second * sine_part, second * cosine + first_half * sine_part],
        axis=-1,
    )


def dot32(a, b):
    return jnp.dot(a, b, preferred_element_type=jnp.float32)


def per_device(
    residual,
    attn_gain,
    w_query,
    w_key,
    value_weight,
    w_out,
    mlp_gain,
    w_gate,
    w_up,
    w_down,
    segment_ids,
    page_table,
):
    rows, cols = lax.axis_size("row"), lax.axis_size("col")
    row_place, col_place = lax.axis_index("row"), lax.axis_index("col")
    lanes = cols // 2
    lane, core = quotient(col_place, 2), remainder(col_place, 2)
    walk = RowWalk(rows)
    row_ring = Ring("row", [walk.listed()], walk.spot_of(row_place))
    lane_ring = Ring("col", [[i * 2 + c for i in range(lanes)] for c in range(2)], lane)
    row_at = [row_place] + [walk.row_at(row_ring.at(i)) for i in range(1, rows)]
    swap = [(i, i ^ 1) for i in range(cols)]

    def other_core(block):
        return lax.ppermute(block, "col", swap)

    tokens = segment_ids.shape[0]
    row_tokens, col_tokens = tokens // rows, tokens // cols
    part_tokens = tokens // PARTS
    row_part, col_part = row_tokens // PARTS, col_tokens // PARTS
    per_col = rows // cols
    row_width = residual.shape[1]
    model_width = row_width * rows
    query_cols, kv_cols = w_query.shape[1], w_key.shape[1]
    kv_local = kv_cols // HEAD_SIZE
    heads = query_cols // HEAD_SIZE
    group = heads // kv_local
    first_row = row_place * row_tokens

    def slot_of_row(who, m):
        if lanes <= 2 and per_col & (per_col - 1) == 0:
            return jnp.bitwise_xor(who, col_place * per_col) * m
        at_col = quotient(who, per_col)
        step = remainder(quotient(at_col, 2) - lane + lanes, lanes)
        side = jnp.bitwise_xor(remainder(at_col, 2), core)
        return ((step * 2 + side) * per_col + remainder(who, per_col)) * m

    def gather_cols(block, after=()):
        near = other_core(block)
        found = sorted(lane_ring.all_gather(block), key=lambda f: f[0] % lanes)
        pieces = [block, near]
        for _, b in found[1:]:
            b = tie(b, *after)
            pieces += [b, other_core(b)]
        return jnp.concatenate(pieces, axis=0), found[-1][1]

    def core_sum(block):
        m, w = block.shape[0] // cols, block.shape[1]
        split = block.reshape(lanes, 2, m, w)
        got = other_core(split[:, 1])
        return (split[:, 0].astype(jnp.float32) + got.astype(jnp.float32)).astype(jnp.bfloat16)

    def lane_walk(summed):
        walk_on = SumWalk(lane_ring, lambda i: summed[i % lanes])
        while walk_on.done < walk_on.steps:
            walk_on.step()
        return walk_on

    def row_blocks(block, m):
        def take(i):
            start = slot_of_row(row_at[i], m)
            return cut_from(block, (start, 0), (m, block.shape[1]))

        return take

    def lay_out(found, along, start_of):
        m, w = found[0][1].shape
        shape = (rows * m, w) if along == 0 else (m, rows * w)
        placed = []
        for i, b in found:
            begin = start_of(row_at[i])
            placed.append(((begin, 0) if along == 0 else (0, begin), b))
        return place_blocks(shape, found[0][1].dtype, placed)

    gathered, _ = gather_cols(residual)
    widened = gathered.astype(jnp.float32)
    scaled = (widened * attn_gain[None, :]).astype(jnp.bfloat16)
    sums = jnp.sum(widened * widened, axis=1)

    kv_terms = jnp.concatenate([dot32(scaled, w_key), dot32(scaled, value_weight)], axis=1)
    kv_terms = kv_terms.astype(jnp.bfloat16)

    late_ids, late_pages, sums = lax.optimization_barrier((segment_ids, page_table, sums, kv_terms))[:3]
    query_index = first_row + jnp.arange(row_tokens, dtype=jnp.int32)
    own_segment = cut_from(late_ids, (first_row,), (row_tokens,))
    seg_starts = jnp.sum((late_ids[None, :] < own_segment[:, None]).astype(jnp.int32), axis=1)
    tables = rotary_tables(query_index - seg_starts)
    key_rows = walk.row_at(remainder(row_ring.spot + jnp.arange(rows, dtype=jnp.int32), rows))
    key_index = key_rows[:, None] * row_tokens + jnp.arange(row_tokens, dtype=jnp.int32)[None, :]
    key_index = key_index.reshape(tokens)
    key_segment = jnp.sum(
        jnp.where(
            key_rows[:, None, None] == jnp.arange(rows, dtype=jnp.int32)[None, :, None],
            late_ids.reshape(1, rows, row_tokens),
            0,
        ),
        axis=1,
    ).reshape(tokens)
    query_terms = dot32(tie(scaled, kv_terms), w_query).astype(jnp.bfloat16)
    query_walk = SumWalk(row_ring, row_blocks(query_terms, row_tokens))
    kv_walk = SumWalk(row_ring, row_blocks(kv_terms, row_tokens))
    kv_spread, bit = None, 1
    for step in range(query_walk.steps):
        query_walk.step()
        for turn in range(2):
            after = ()
            if kv_walk.done < kv_walk.steps:
                kv_walk.step(after)
                if bit < rows:
                    got = lax.ppermute(sums, "row", [(i, i ^ bit) for i in range(rows)])
                    sums = sums + tie(got, *kv_walk.got)
                    bit *= 2
                continue
            if kv_spread is None:
                attn_scale = lax.rsqrt(
                    cut_from(sums, (slot_of_row(row_place, row_tokens),), (row_tokens,)) / model_width
                    + EPSILON
                )[:, None]
                kv_own = kv_walk.result() * attn_scale
                key_own = rotary_apply(
                    kv_own[:, :kv_cols].reshape(row_tokens, kv_local, HEAD_SIZE), tables
                ).reshape(row_tokens, kv_cols)
                key_value = jnp.concatenate([key_own, kv_own[:, kv_cols:]], axis=1)
                kv_spread = GatherWalk(row_ring, key_value.astype(jnp.bfloat16))
            kv_spread.step(after)
    found = sorted(kv_spread.run(), key=lambda f: f[0] % rows)
    key_value = jnp.concatenate([b for _, b in found], axis=0)
    key_all, value_all = key_value[:, :kv_cols], key_value[:, kv_cols:]
    key_heads = key_all.reshape(tokens, kv_local, HEAD_SIZE)
    value_heads = value_all.reshape(tokens, kv_local, HEAD_SIZE)

    queries = query_walk.result() * attn_scale
    queries = rotary_apply(queries.reshape(row_tokens, heads, HEAD_SIZE), tables)
    queries = queries.astype(jnp.bfloat16)

    def attend(part, after=()):
        own = slice(part * row_part, (part + 1) * row_part)
        key_mask = (
            (key_segment[None, :] == own_segment[own][:, None])
            & (key_index[None, :] <= query_index[own][:, None])
        )[None, None]
        scores = jnp.where(
            key_mask,
            jnp.einsum(
                "tjgd,sjd->jgts",
                tie(queries[own], *after).reshape(row_part, kv_local, group, HEAD_SIZE),
                key_heads,
                preferred_element_type=jnp.float32,
            )
            * HEAD_SIZE ** (-0.5),
            NEGATIVE,
        )
        peak_score = jnp.max(scores, axis=3, keepdims=True)
        weights = jnp.where(key_mask, jnp.exp(scores - peak_score), 0.0).astype(jnp.bfloat16)
        weight_sum = jnp.sum(weights.astype(jnp.float32), axis=3)
        mixture = jnp.einsum(
            "jgts,sjd->jgtd", weights, value_heads, preferred_element_type=jnp.float32
        )
        return (
            jnp.transpose(mixture / weight_sum[..., None], (2, 0, 1, 3))
            .reshape(row_part, query_cols)
            .astype(jnp.bfloat16)
        )

    def head_sums(walk_on):
        attended = lay_out(walk_on.found, 0, lambda who: slot_of_row(who, row_part))
        return core_sum(dot32(attended, w_out).astype(jnp.bfloat16))

    def add_stream(part, summed):
        own = residual.reshape(per_col, PARTS, row_part, row_width)[:, part]
        own = own.reshape(col_part, row_width).astype(jnp.float32)
        return GatherWalk(row_ring, (own + lane_walk(summed).result()).astype(jnp.bfloat16))

    def spread(full_rows):
        w = model_width // cols
        span = 2 * w
        mine = [(0, cut_from(full_rows, (0, lane * span), (col_part, span)))]
        for hop in range(1, lanes):
            pairs = [
                (i * 2 + c, ((i + hop) % lanes) * 2 + c) for i in range(lanes) for c in range(2)
            ]
            sent = cut_from(full_rows, (0, lane_ring.at(hop) * span), (col_part, span))
            mine.append((-hop % lanes, lax.ppermute(sent, "col", pairs)))
        return [b for _, b in sorted(mine, key=lambda f: f[0])]

    def scale_of(blocks):
        total = 0.0
        for block in blocks:
            block = block.astype(jnp.float32)
            total = total + jnp.sum(block * block, axis=1)
        return lax.rsqrt(total / model_width + EPSILON)[:, None]

    def along_z(block, last_after):
        up = [(z * 2 + x, (z + 1) % 4 * 2 + x) for z in range(4) for x in range(2)]
        blocks = [block]
        while len(blocks) < 4:
            after = last_after if len(blocks) == LAST else ()
            blocks.append(lax.ppermute(tie(blocks[-1], *after), "row", up))
        return blocks

    def to_takers(blocks):
        z = quotient(row_place, 2)
        here = [quotient(remainder(z - i + 4, 4), 2) == lane for i in range(2)]
        given = [jnp.where(here[i], blocks[i + 2], blocks[i]) for i in range(2)]
        kept = [jnp.where(here[i], blocks[i], blocks[i + 2]) for i in range(2)]
        over = lax.ppermute(jnp.concatenate(given, axis=0), "col", [(i, i ^ 2) for i in range(cols)])
        came = [over[:col_part], over[col_part:]]
        first = remainder(jnp.bitwise_xor(z, core), 2) == 0
        mine = [jnp.where(first, b[0], b[1]) for b in (kept, came)]
        theirs = [jnp.where(first, b[1], b[0]) for b in (kept, came)]
        near = other_core(jnp.concatenate(theirs, axis=0))
        return jnp.concatenate([mine[0], near[:col_part], mine[1], near[col_part:]], axis=0)

    def join_x(own, other):
        x = remainder(row_place, 2)
        return jnp.concatenate(
            [jnp.where(x == 0, own, other), jnp.where(x == 0, other, own)], axis=1
        )

    def join_cores(mine, before_core):
        w = model_width // cols
        pieces = []
        for hop, b in enumerate(mine):
            if hop:
                b = tie(b, *before_core)
            sent = cut_from(b, (0, (1 - core) * w), (col_part, w))
            pieces += [cut_from(b, (0, core * w), (col_part, w)), other_core(sent)]
        return jnp.concatenate(pieces, axis=0)

    def widen(stream):
        mid = (stream.astype(jnp.float32) * mlp_gain[None, :]).astype(jnp.bfloat16)
        mid = lax.optimization_barrier(mid)
        gate = dot32(mid, w_gate).astype(jnp.bfloat16)
        up = dot32(mid, w_up).astype(jnp.bfloat16)
        return core_sum(gate), core_sum(up), (gate, up)

    block_0 = attend(0)
    heads_0 = GatherWalk(row_ring, block_0)
    heads_0.step()
    block_1 = attend(1, (block_0,))
    heads_1 = GatherWalk(row_ring, block_1)
    heads_0.step((block_1,))
    steps = heads_0.steps
    for step in range(2, steps):
        heads_0.step()
        heads_1.step(heads_0.found[-4][1:] if step == 2 else ())
    summed_0 = head_sums(heads_0)
    stream_0 = add_stream(0, summed_0)
    while heads_1.done < steps:
        heads_1.step((summed_0,) if heads_1.done == steps - 1 else ())
    stream_0.step()
    stream_0.step()
    second = stream_0.got
    full = lay_out(stream_0.run(), 1, lambda who: who * row_width)
    scales = [scale_of([full])]
    halves = spread(full)
    stream_1 = add_stream(1, head_sums(heads_1))
    if rows == 8 and cols == 4:
        swap_x = [(i, i ^ 1) for i in range(rows)]
        blocks = along_z(tie(stream_1.found[0][1], *second), halves[1:])
        total = 0.0
        for block in blocks:
            block = block.astype(jnp.float32)
            total = total + jnp.sum(block * block, axis=1)
        total = total + lax.ppermute(total, "row", swap_x)
        scales.append(lax.rsqrt(total / model_width + EPSILON)[:, None])
        own = to_takers(blocks)
        other = lax.ppermute(own, "row", swap_x)
        stream_0 = join_cores(halves, ())
        gate_0, up_0, terms_0 = widen(stream_0)
        stream_1 = join_x(own, tie(other, *terms_0))
    else:
        stream_1.step(second)
        full = lay_out(stream_1.run(), 1, lambda who: who * row_width)
        scales.append(scale_of([full]))
        stream_0 = join_cores(halves, ())
        gate_0, up_0, terms_0 = widen(stream_0)
        stream_1 = join_cores(spread(full), terms_0)

    def gated(gate, up, scale):
        return (jax.nn.silu(gate * scale) * (up * scale)).astype(jnp.bfloat16)

    def down_walk(everyone):
        down = dot32(everyone, w_down).astype(jnp.bfloat16)
        return SumWalk(row_ring, row_blocks(down, row_part))

    def finish(stream, walk_on):
        own = cut_from(stream, (slot_of_row(row_place, row_part), 0), (row_part, stream.shape[1]))
        return (own.astype(jnp.float32) + walk_on.result()).astype(jnp.bfloat16)

    gate_0, up_0 = lane_walk(gate_0), lane_walk(up_0)
    gate_1, up_1, terms_1 = widen(tie(stream_1, *gate_0.got))
    hidden_0 = gated(gate_0.result(), up_0.result(), scales[0])
    everyone, far = gather_cols(hidden_0, terms_1)
    gate_1, up_1 = lane_walk(tie(gate_1, far)), lane_walk(tie(up_1, far))
    down_0 = down_walk(everyone)
    while down_0.done < down_0.steps - 1:
        down_0.step()
    gate_1.got, up_1.got = tie_all(gate_1.got, down_0.got), tie_all(up_1.got, down_0.got)
    gate_1, up_1 = gate_1.result(), up_1.result()
    down_0.step()
    everyone, far = gather_cols(gated(gate_1, up_1, scales[1]), down_0.got)
    down_1 = down_walk(everyone)
    down_1.run()
    output = jnp.concatenate([finish(stream_0, down_0), finish(stream_1, down_1)], axis=0)

    block_count = page_table.shape[0]
    page_size = tokens // block_count
    slots_local = block_count // rows
    slot_ids = row_place * slots_local + jnp.arange(slots_local, dtype=jnp.int32)
    block_ids = jnp.arange(block_count, dtype=jnp.int32)
    owned_blocks = jnp.sum(
        jnp.where(late_pages[None, :] == slot_ids[:, None], block_ids[None, :], 0), axis=1
    )
    row_blocks_count = block_count // rows
    at_row = quotient(owned_blocks, row_blocks_count)
    away = remainder(walk.spot_of(at_row) - row_ring.spot + rows, rows)
    owned_blocks = away * row_blocks_count + remainder(owned_blocks, row_blocks_count)
    page_rows = owned_blocks[:, None] * page_size + jnp.arange(page_size, dtype=jnp.int32)[None, :]
    key_cache_pages = jnp.take(key_all, page_rows, axis=0)
    value_cache_pages = jnp.take(value_all, page_rows, axis=0)
    return (output, key_cache_pages, value_cache_pages)


def solution(mesh):
    return jax.shard_map(
        per_device,
        mesh=mesh,
        in_specs=(
            P("col", "row"),
            P("row"),
            P("row", "col"),
            P("row", "col"),
            P("row", "col"),
            P("col", "row"),
            P("col"),
            P("col", "row"),
            P("col", "row"),
            P("row", "col"),
            P(),
            P(),
        ),
        out_specs=(P("row", "col"), P("row", None, "col"), P("row", None, "col")),
        check_vma=False,
    )
```

```python
import jax
import jax.numpy as jnp
from jax import lax
from jax.sharding import PartitionSpec as P

HEAD_SIZE = 128
ROPE_BASE = 5000000.0
EPSILON = 1e-05
NEGATIVE = -1e30
PARTS = 2
LAST = 3
LAG = 2


def quotient(value, size):
    if size & (size - 1):
        return lax.div(value, jnp.int32(size))
    return lax.shift_right_logical(value, jnp.int32(size.bit_length() - 1)) if size > 1 else value


def remainder(value, size):
    if size & (size - 1):
        return lax.rem(value, jnp.int32(size))
    return jnp.bitwise_and(value, jnp.int32(size - 1))


def cut_from(block, start, sizes):
    return lax.dynamic_slice(block, start, sizes, allow_negative_indices=False)


class RowWalk:
    def __init__(self, rows):
        self.depth = 4 if rows % 4 == 0 else 1
        self.width = rows // self.depth
        self.rows = rows

    def turned(self, x, z):
        if self.depth & (self.depth - 1) == 0 and self.width == 2:
            return jnp.bitwise_xor(z, x * (self.depth - 1))
        return jnp.where(remainder(x, 2) == 1, self.depth - 1 - z, z)

    def row_at(self, spot):
        x = quotient(spot, self.depth)
        return self.turned(x, remainder(spot, self.depth)) * self.width + x

    def spot_of(self, row):
        x = remainder(row, self.width)
        return x * self.depth + self.turned(x, quotient(row, self.width))

    def listed(self):
        walk = []
        for x in range(self.width):
            zs = range(self.depth) if x % 2 == 0 else reversed(range(self.depth))
            walk += [z * self.width + x for z in zs]
        return walk


class Ring:
    def __init__(self, axis, walks, spot):
        self.axis = axis
        self.size = n = len(walks[0])
        self.right = [(w[i], w[(i + 1) % n]) for w in walks for i in range(n)]
        self.left = [(w[(i + 1) % n], w[i]) for w in walks for i in range(n)]
        self.spot = spot

    def send(self, block, pairs):
        return lax.ppermute(block, self.axis, pairs)

    def at(self, offset):
        return remainder(self.spot + offset % self.size, self.size) if offset % self.size else self.spot

    def reduce_scatter(self, take):
        return SumWalk(self, take).run()

    def all_gather(self, block):
        return GatherWalk(self, block).run()


class SumWalk:
    def __init__(self, ring, take):
        self.ring, self.take, self.done = ring, take, 0
        self.steps = ring.size // 2
        self.sent = self.got = ()

    def step(self, after=()):
        ring, take, half = self.ring, self.take, self.steps
        self.done += 1
        if ring.size == 2:
            right, left = take(1).astype(jnp.bfloat16), None
        elif self.done == 1:
            far = take(half).astype(jnp.bfloat16)
            self.cut = far.shape[0] // 2
            right, left = far[: self.cut], far[self.cut :]
        else:
            place = half - self.done + 1
            right = take(place).astype(jnp.float32)
            left = take(-place).astype(jnp.float32)
            going_right, going_left = (g.astype(jnp.float32) for g in self.got)
            if self.done == 2:
                cut = self.cut
                right = jnp.concatenate([right[:cut] + going_right, right[cut:]], axis=0)
                left = jnp.concatenate([left[:cut], left[cut:] + going_left], axis=0)
            else:
                right, left = right + going_right, left + going_left
            right, left = right.astype(jnp.bfloat16), left.astype(jnp.bfloat16)
        if left is None:
            self.sent = (tie(right, *after),)
            self.got = (ring.send(self.sent[0], ring.right),)
        else:
            self.sent = tie_all((right, left), after)
            self.got = (ring.send(self.sent[0], ring.right), ring.send(self.sent[1], ring.left))

    def result(self):
        total = self.take(0).astype(jnp.float32)
        for block in self.got:
            total = total + block.astype(jnp.float32)
        return total

    def run(self):
        while self.done < self.steps:
            self.step()
        return self.result()


class GatherWalk:
    def __init__(self, ring, block):
        self.ring, self.done = ring, 0
        self.steps = ring.size // 2
        self.found = [(0, block)]
        self.got = (block, block)

    def step(self, after=()):
        ring = self.ring
        self.done += 1
        if ring.size == 2:
            self.got = (ring.send(tie(self.got[0], *after), ring.right),)
            self.found.append((1, self.got[0]))
            return
        right, left = tie_all(self.got, after)
        if self.done == self.steps:
            cut = right.shape[0] // 2
            right, left = right[:cut], left[cut:]
        self.got = (ring.send(right, ring.right), ring.send(left, ring.left))
        if self.done == self.steps:
            self.found.append((self.done, jnp.concatenate(self.got, axis=0)))
        else:
            self.found += [(-self.done, self.got[0]), (self.done, self.got[1])]

    def run(self):
        while self.done < self.steps:
            self.step()
        return self.found


def tie_all(blocks, earlier):
    if len(blocks) + len(earlier) < 2:
        return tuple(blocks)
    return tuple(lax.optimization_barrier((*blocks, *earlier))[: len(blocks)])


def tie(block, *earlier):
    return tie_all((block,), earlier)[0]


def place_blocks(shape, dtype, placed):
    buffer = jnp.zeros(shape, dtype)
    for start, block in placed:
        buffer = lax.dynamic_update_slice(buffer, block, start, allow_negative_indices=False)
    return buffer


def rotary_tables(token_positions):
    half_width = HEAD_SIZE // 2
    frequency = ROPE_BASE ** (-2.0 * jnp.arange(half_width, dtype=jnp.float32) / HEAD_SIZE)
    angles = token_positions.astype(jnp.float32)[:, None] * frequency[None, :]
    return jnp.cos(angles)[:, None, :], jnp.sin(angles)[:, None, :]


def rotary_apply(block, tables):
    cosine, sine_part = tables
    half_width = block.shape[-1] // 2
    first_half = block[..., :half_width]
    second = block[..., half_width:]
    return jnp.concatenate(
        [first_half * cosine - second * sine_part, second * cosine + first_half * sine_part],
        axis=-1,
    )


def dot32(a, b):
    return jnp.dot(a, b, preferred_element_type=jnp.float32)


def per_device(
    residual,
    attn_gain,
    w_query,
    w_key,
    value_weight,
    w_out,
    mlp_gain,
    w_gate,
    w_up,
    w_down,
    segment_ids,
    page_table,
):
    rows, cols = lax.axis_size("row"), lax.axis_size("col")
    row_place, col_place = lax.axis_index("row"), lax.axis_index("col")
    lanes = cols // 2
    lane, core = quotient(col_place, 2), remainder(col_place, 2)
    walk = RowWalk(rows)
    row_ring = Ring("row", [walk.listed()], walk.spot_of(row_place))
    lane_ring = Ring("col", [[i * 2 + c for i in range(lanes)] for c in range(2)], lane)
    row_at = [row_place] + [walk.row_at(row_ring.at(i)) for i in range(1, rows)]
    swap = [(i, i ^ 1) for i in range(cols)]

    def other_core(block):
        return lax.ppermute(block, "col", swap)

    tokens = segment_ids.shape[0]
    row_tokens, col_tokens = tokens // rows, tokens // cols
    part_tokens = tokens // PARTS
    row_part, col_part = row_tokens // PARTS, col_tokens // PARTS
    per_col = rows // cols
    row_width = residual.shape[1]
    model_width = row_width * rows
    query_cols, kv_cols = w_query.shape[1], w_key.shape[1]
    kv_local = kv_cols // HEAD_SIZE
    heads = query_cols // HEAD_SIZE
    group = heads // kv_local
    first_row = row_place * row_tokens

    def slot_of_row(who, m):
        if lanes <= 2 and per_col & (per_col - 1) == 0:
            return jnp.bitwise_xor(who, col_place * per_col) * m
        at_col = quotient(who, per_col)
        step = remainder(quotient(at_col, 2) - lane + lanes, lanes)
        side = jnp.bitwise_xor(remainder(at_col, 2), core)
        return ((step * 2 + side) * per_col + remainder(who, per_col)) * m

    def gather_cols(block, after=()):
        near = other_core(block)
        found = sorted(lane_ring.all_gather(block), key=lambda f: f[0] % lanes)
        pieces = [block, near]
        for _, b in found[1:]:
            b = tie(b, *after)
            pieces += [b, other_core(b)]
        return jnp.concatenate(pieces, axis=0), found[-1][1]

    def core_sum(block):
        m, w = block.shape[0] // cols, block.shape[1]
        split = block.reshape(lanes, 2, m, w)
        got = other_core(split[:, 1])
        return (split[:, 0].astype(jnp.float32) + got.astype(jnp.float32)).astype(jnp.bfloat16)

    def lane_walk(summed):
        walk_on = SumWalk(lane_ring, lambda i: summed[i % lanes])
        while walk_on.done < walk_on.steps:
            walk_on.step()
        return walk_on

    def row_blocks(block, m):
        def take(i):
            start = slot_of_row(row_at[i], m)
            return cut_from(block, (start, 0), (m, block.shape[1]))

        return take

    def lay_out(found, along, start_of):
        m, w = found[0][1].shape
        shape = (rows * m, w) if along == 0 else (m, rows * w)
        placed = []
        for i, b in found:
            begin = start_of(row_at[i])
            placed.append(((begin, 0) if along == 0 else (0, begin), b))
        return place_blocks(shape, found[0][1].dtype, placed)

    gathered, _ = gather_cols(residual)
    widened = gathered.astype(jnp.float32)
    scaled = (widened * attn_gain[None, :]).astype(jnp.bfloat16)
    sums = jnp.sum(widened * widened, axis=1)

    kv_terms = jnp.concatenate([dot32(scaled, w_key), dot32(scaled, value_weight)], axis=1)
    kv_terms = kv_terms.astype(jnp.bfloat16)

    late_ids, late_pages, sums = lax.optimization_barrier((segment_ids, page_table, sums, kv_terms))[:3]
    query_index = first_row + jnp.arange(row_tokens, dtype=jnp.int32)
    own_segment = cut_from(late_ids, (first_row,), (row_tokens,))
    seg_starts = jnp.sum((late_ids[None, :] < own_segment[:, None]).astype(jnp.int32), axis=1)
    tables = rotary_tables(query_index - seg_starts)
    key_rows = walk.row_at(remainder(row_ring.spot + jnp.arange(rows, dtype=jnp.int32), rows))
    key_index = key_rows[:, None] * row_tokens + jnp.arange(row_tokens, dtype=jnp.int32)[None, :]
    key_index = key_index.reshape(tokens)
    key_segment = jnp.sum(
        jnp.where(
            key_rows[:, None, None] == jnp.arange(rows, dtype=jnp.int32)[None, :, None],
            late_ids.reshape(1, rows, row_tokens),
            0,
        ),
        axis=1,
    ).reshape(tokens)
    query_terms = dot32(tie(scaled, kv_terms), w_query).astype(jnp.bfloat16)
    query_walk = SumWalk(row_ring, row_blocks(query_terms, row_tokens))
    kv_walk = SumWalk(row_ring, row_blocks(kv_terms, row_tokens))
    kv_spread, bit = None, 1
    for step in range(query_walk.steps):
        query_walk.step()
        for turn in range(2):
            after = ()
            if kv_walk.done < kv_walk.steps:
                kv_walk.step(after)
                if bit < rows:
                    got = lax.ppermute(sums, "row", [(i, i ^ bit) for i in range(rows)])
                    sums = sums + tie(got, *kv_walk.got)
                    bit *= 2
                continue
            if kv_spread is None:
                attn_scale = lax.rsqrt(
                    cut_from(sums, (slot_of_row(row_place, row_tokens),), (row_tokens,)) / model_width
                    + EPSILON
                )[:, None]
                kv_own = kv_walk.result() * attn_scale
                key_own = rotary_apply(
                    kv_own[:, :kv_cols].reshape(row_tokens, kv_local, HEAD_SIZE), tables
                ).reshape(row_tokens, kv_cols)
                key_value = jnp.concatenate([key_own, kv_own[:, kv_cols:]], axis=1)
                kv_spread = GatherWalk(row_ring, key_value.astype(jnp.bfloat16))
            kv_spread.step(after)
    found = sorted(kv_spread.run(), key=lambda f: f[0] % rows)
    key_value = jnp.concatenate([b for _, b in found], axis=0)
    key_all, value_all = key_value[:, :kv_cols], key_value[:, kv_cols:]
    key_heads = key_all.reshape(tokens, kv_local, HEAD_SIZE)
    value_heads = value_all.reshape(tokens, kv_local, HEAD_SIZE)

    queries = query_walk.result() * attn_scale
    queries = rotary_apply(queries.reshape(row_tokens, heads, HEAD_SIZE), tables)
    queries = queries.astype(jnp.bfloat16)

    def attend(part, after=()):
        own = slice(part * row_part, (part + 1) * row_part)
        key_mask = (
            (key_segment[None, :] == own_segment[own][:, None])
            & (key_index[None, :] <= query_index[own][:, None])
        )[None, None]
        scores = jnp.where(
            key_mask,
            jnp.einsum(
                "tjgd,sjd->jgts",
                tie(queries[own], *after).reshape(row_part, kv_local, group, HEAD_SIZE),
                key_heads,
                preferred_element_type=jnp.float32,
            )
            * HEAD_SIZE ** (-0.5),
            NEGATIVE,
        )
        peak_score = jnp.max(scores, axis=3, keepdims=True)
        weights = jnp.where(key_mask, jnp.exp(scores - peak_score), 0.0).astype(jnp.bfloat16)
        weight_sum = jnp.sum(weights.astype(jnp.float32), axis=3)
        mixture = jnp.einsum(
            "jgts,sjd->jgtd", weights, value_heads, preferred_element_type=jnp.float32
        )
        return (
            jnp.transpose(mixture / weight_sum[..., None], (2, 0, 1, 3))
            .reshape(row_part, query_cols)
            .astype(jnp.bfloat16)
        )

    def head_sums(walk_on):
        attended = lay_out(walk_on.found, 0, lambda who: slot_of_row(who, row_part))
        return core_sum(dot32(attended, w_out).astype(jnp.bfloat16))

    def add_stream(part, summed):
        own = residual.reshape(per_col, PARTS, row_part, row_width)[:, part]
        own = own.reshape(col_part, row_width).astype(jnp.float32)
        return GatherWalk(row_ring, (own + lane_walk(summed).result()).astype(jnp.bfloat16))

    def spread(full_rows):
        w = model_width // cols
        span = 2 * w
        mine = [(0, cut_from(full_rows, (0, lane * span), (col_part, span)))]
        for hop in range(1, lanes):
            pairs = [
                (i * 2 + c, ((i + hop) % lanes) * 2 + c) for i in range(lanes) for c in range(2)
            ]
            sent = cut_from(full_rows, (0, lane_ring.at(hop) * span), (col_part, span))
            mine.append((-hop % lanes, lax.ppermute(sent, "col", pairs)))
        return [b for _, b in sorted(mine, key=lambda f: f[0])]

    def scale_of(blocks):
        total = 0.0
        for block in blocks:
            block = block.astype(jnp.float32)
            total = total + jnp.sum(block * block, axis=1)
        return lax.rsqrt(total / model_width + EPSILON)[:, None]

    def along_z(block, last_after):
        up = [(z * 2 + x, (z + 1) % 4 * 2 + x) for z in range(4) for x in range(2)]
        blocks = [block]
        while len(blocks) < 4:
            after = last_after if len(blocks) == LAST else ()
            blocks.append(lax.ppermute(tie(blocks[-1], *after), "row", up))
        return blocks

    def to_takers(blocks, after):
        z = quotient(row_place, 2)
        here = [quotient(remainder(z - i + 4, 4), 2) == lane for i in range(2)]
        given = [jnp.where(here[i], blocks[i + 2], blocks[i]) for i in range(2)]
        kept = [jnp.where(here[i], blocks[i], blocks[i + 2]) for i in range(2)]
        given = tie(jnp.concatenate(given, axis=0), *after)
        over = lax.ppermute(given, "col", [(i, i ^ 2) for i in range(cols)])
        came = [over[:col_part], over[col_part:]]
        first = remainder(jnp.bitwise_xor(z, core), 2) == 0
        mine = [jnp.where(first, b[0], b[1]) for b in (kept, came)]
        theirs = [jnp.where(first, b[1], b[0]) for b in (kept, came)]
        near = other_core(jnp.concatenate(theirs, axis=0))
        return jnp.concatenate([mine[0], near[:col_part], mine[1], near[col_part:]], axis=0)

    def join_x(own, other):
        x = remainder(row_place, 2)
        return jnp.concatenate(
            [jnp.where(x == 0, own, other), jnp.where(x == 0, other, own)], axis=1
        )

    def join_cores(mine, before_core):
        w = model_width // cols
        pieces = []
        for hop, b in enumerate(mine):
            if hop:
                b = tie(b, *before_core)
            sent = cut_from(b, (0, (1 - core) * w), (col_part, w))
            pieces += [cut_from(b, (0, core * w), (col_part, w)), other_core(sent)]
        return jnp.concatenate(pieces, axis=0)

    def widen(stream):
        mid = (stream.astype(jnp.float32) * mlp_gain[None, :]).astype(jnp.bfloat16)
        mid = lax.optimization_barrier(mid)
        gate = dot32(mid, w_gate).astype(jnp.bfloat16)
        up = dot32(mid, w_up).astype(jnp.bfloat16)
        return core_sum(gate), core_sum(up), (gate, up)

    block_0 = attend(0)
    heads_0 = GatherWalk(row_ring, block_0)
    heads_0.step()
    block_1 = attend(1, (block_0,))
    heads_1 = GatherWalk(row_ring, block_1)
    heads_0.step((block_1,))
    steps = heads_0.steps
    for step in range(2, steps):
        heads_0.step()
        heads_1.step(heads_0.found[-4][1:] if step == 2 else ())
    summed_0 = head_sums(heads_0)
    stream_0 = add_stream(0, summed_0)
    while heads_1.done < steps:
        heads_1.step((summed_0,) if heads_1.done == steps - 1 else ())
    stream_0.step()
    stream_0.step()
    second = stream_0.got
    full = lay_out(stream_0.run(), 1, lambda who: who * row_width)
    scales = [scale_of([full])]
    halves = spread(full)
    stream_1 = add_stream(1, head_sums(heads_1))
    if rows == 8 and cols == 4:
        swap_x = [(i, i ^ 1) for i in range(rows)]
        blocks = along_z(tie(stream_1.found[0][1], *second), halves[1:])
        total = 0.0
        for block in blocks:
            block = block.astype(jnp.float32)
            total = total + jnp.sum(block * block, axis=1)
        total = total + lax.ppermute(total, "row", swap_x)
        scales.append(lax.rsqrt(total / model_width + EPSILON)[:, None])
        stream_0 = join_cores(halves, ())
        gate_0, up_0, terms_0 = widen(stream_0)
        own = to_takers(blocks, terms_0[:1])
        other = lax.ppermute(own, "row", swap_x)
        stream_1 = join_x(own, tie(other, *terms_0))
    else:
        stream_1.step(second)
        full = lay_out(stream_1.run(), 1, lambda who: who * row_width)
        scales.append(scale_of([full]))
        stream_0 = join_cores(halves, ())
        gate_0, up_0, terms_0 = widen(stream_0)
        stream_1 = join_cores(spread(full), terms_0)

    def gated(gate, up, scale):
        return (jax.nn.silu(gate * scale) * (up * scale)).astype(jnp.bfloat16)

    def down_walk(everyone):
        down = dot32(everyone, w_down).astype(jnp.bfloat16)
        return SumWalk(row_ring, row_blocks(down, row_part))

    def finish(stream, walk_on):
        own = cut_from(stream, (slot_of_row(row_place, row_part), 0), (row_part, stream.shape[1]))
        return (own.astype(jnp.float32) + walk_on.result()).astype(jnp.bfloat16)

    gate_0, up_0 = lane_walk(gate_0), lane_walk(up_0)
    gate_1, up_1, terms_1 = widen(tie(stream_1, *gate_0.got))
    hidden_0 = gated(gate_0.result(), up_0.result(), scales[0])
    everyone, far = gather_cols(hidden_0, terms_1)
    gate_1, up_1 = lane_walk(gate_1), lane_walk(tie(up_1, far))
    down_0 = down_walk(everyone)
    while down_0.done < down_0.steps - 1:
        down_0.step()
    gate_1.got, up_1.got = tie_all(gate_1.got, down_0.got), tie_all(up_1.got, down_0.got)
    gate_1, up_1 = gate_1.result(), up_1.result()
    down_0.step()
    everyone, far = gather_cols(gated(gate_1, up_1, scales[1]), down_0.got)
    down_1 = down_walk(everyone)
    down_1.run()
    output = jnp.concatenate([finish(stream_0, down_0), finish(stream_1, down_1)], axis=0)

    block_count = page_table.shape[0]
    page_size = tokens // block_count
    slots_local = block_count // rows
    slot_ids = row_place * slots_local + jnp.arange(slots_local, dtype=jnp.int32)
    block_ids = jnp.arange(block_count, dtype=jnp.int32)
    owned_blocks = jnp.sum(
        jnp.where(late_pages[None, :] == slot_ids[:, None], block_ids[None, :], 0), axis=1
    )
    row_blocks_count = block_count // rows
    at_row = quotient(owned_blocks, row_blocks_count)
    away = remainder(walk.spot_of(at_row) - row_ring.spot + rows, rows)
    owned_blocks = away * row_blocks_count + remainder(owned_blocks, row_blocks_count)
    page_rows = owned_blocks[:, None] * page_size + jnp.arange(page_size, dtype=jnp.int32)[None, :]
    key_cache_pages = jnp.take(key_all, page_rows, axis=0)
    value_cache_pages = jnp.take(value_all, page_rows, axis=0)
    return (output, key_cache_pages, value_cache_pages)


def solution(mesh):
    return jax.shard_map(
        per_device,
        mesh=mesh,
        in_specs=(
            P("col", "row"),
            P("row"),
            P("row", "col"),
            P("row", "col"),
            P("row", "col"),
            P("col", "row"),
            P("col"),
            P("col", "row"),
            P("col", "row"),
            P("row", "col"),
            P(),
            P(),
        ),
        out_specs=(P("row", "col"), P("row", None, "col"), P("row", None, "col")),
        check_vma=False,
    )
```
